128 devices in a mesh: dp: 4 (over y_lo, core), mp: 32 (over y_hi, z, x).
Axes of the slice: x: 4, y: 4 (y_hi: 2, y_lo: 2; y = y_hi * 2 + y_lo), z: 4, core: 2. Of those that a mesh axis runs over, the one named last changes fastest.
Arguments:
- inputs: bfloat16 [512, 8192], P(None, ('dp', 'mp')), may hold values from -6 to 6
- grad_out: bfloat16 [512, 8192], P(None, ('dp', 'mp')), may hold values from -6 to 6
- gate_weight: bfloat16 [8192, 28672], P('dp', 'mp'), may hold values from -0.125 to 0.125
- up_weight: bfloat16 [8192, 28672], P('dp', 'mp'), may hold values from -0.125 to 0.125
- down_weight: bfloat16 [28672, 8192], P('mp', 'dp'), may hold values from -0.03125 to 0.03125
Outputs:
- grad_inputs: bfloat16 [512, 8192], P(None, ('dp', 'mp'))
- grad_gate: bfloat16 [8192, 28672], P('dp', 'mp')
- grad_up: bfloat16 [8192, 28672], P('dp', 'mp')
- grad_down: bfloat16 [28672, 8192], P('mp', 'dp')
The draws below stay inside these ranges and needn't reach their ends.
All inputs are finite; a program needn't handle non-finite values.
Results may differ from the reference program's by a relative error of at most 0.0014.
Values may be sent and summed in bfloat16 or wider, within the bound.
No kernel may reach another device: no remote copies, remote signals or barrier semaphores. Data moves between devices by JAX's collectives and lax.ppermute only.
A program may use at most 128 MiB of HBM per device.

```python
import jax
import jax.numpy as jnp
from jax import lax

D = 8192
FF = 28672
TOKENS = 512
N_MP = 32


def spiked(result, own_key, source, target, parts, factor):
    def block_of(position):
        return (jnp.arange(result.shape[position]) // (result.shape[position] // parts)).reshape((-1,) + (1,) * (result.ndim - 1 - position))

    one_side = jax.random.permutation(own_key, parts)[block_of(target)]
    other_side = (block_of(target) + parts // 2) % parts
    return jnp.where((block_of(source) == one_side) | (block_of(source) == other_side), factor * result, result)


def steps_of(own_key, extent, pieces, low, top_value):
    loudness, own = 1.0, jax.random.fold_in(own_key, 6)
    for axis_at, shards_of in pieces:
        steps = jnp.exp(jax.random.uniform(jax.random.fold_in(own, axis_at), (shards_of,), jnp.float32, low / len(pieces), top_value / len(pieces)))
        loudness = loudness * jnp.repeat(steps, extent[axis_at] // shards_of).reshape([-1 if axis == axis_at else 1 for axis in range(len(extent))])
    return loudness


def noise(key, dims, scale, bound, cuts=(), kind=jnp.bfloat16):
    gain = steps_of(key, dims, cuts, -0.22, 0.18) if cuts else 1.0
    values = jax.random.normal(key, dims, jnp.float32) * scale * gain
    return jnp.minimum(jnp.maximum(values, -bound), bound).astype(kind)


def gaussian_with(stream_key, extent, spread, reach, split, heavy, kind=jnp.bfloat16):
    entries = spread * jax.random.normal(stream_key, extent, jnp.float32)
    if split:
        entries = entries * steps_of(stream_key, extent, split, -0.22, 0.18)
    return jnp.clip(spiked(entries, jax.random.fold_in(stream_key, 3), *heavy), -reach, reach).astype(kind)


def setup_inputs(seed: int = 0) -> dict:
    seeds = jax.random.split(jax.random.key(seed), 6)
    inputs = noise(seeds[0], (TOKENS, D), 1.0, 6.0, ((1, 128),))
    grad_out = noise(seeds[1], (TOKENS, D), 1.0, 6.0, ((1, 128),))
    gate_weight = gaussian_with(seeds[2], (D, FF), D ** -0.5, 0.125, ((0, 4), (1, 32)), (1, 0, 32, 2.75))
    up_weight = gaussian_with(seeds[3], (D, FF), D ** -0.5, 0.125, ((0, 4), (1, 32)), (1, 0, 32, 2.75))
    down_weight = noise(seeds[4], (FF, D), FF ** -0.5, 0.03125, ((0, 32), (1, 4)))
    return {"inputs": inputs, "grad_out": grad_out, "gate_weight": gate_weight, "up_weight": up_weight, "down_weight": down_weight}


HIGH = lax.Precision.HIGHEST


def reference(inputs, grad_out, gate_weight, up_weight, down_weight):
    blocks = N_MP
    width = FF // blocks
    gate_blocks = jnp.moveaxis(gate_weight.reshape(D, blocks, width), 1, 0)
    up_blocks = jnp.moveaxis(up_weight.reshape(D, blocks, width), 1, 0)
    down_blocks = down_weight.reshape(blocks, width, D)
    wide_inputs = inputs.astype(jnp.float32)
    wide_grads = grad_out.astype(jnp.float32)

    def one_block(carry, weights):
        w_gate, w_up, w_down = weights
        gate = jnp.dot(inputs, w_gate, preferred_element_type=jnp.float32)
        up = jnp.dot(inputs, w_up, preferred_element_type=jnp.float32)
        grad_hidden = lax.dot_general(grad_out, w_down, (((1,), (1,)), ((), ())), preferred_element_type=jnp.float32)
        squash = jax.nn.sigmoid(gate)
        hidden = gate * squash * up
        up_delta = grad_hidden * gate * squash
        gate_delta = grad_hidden * up * squash * (1.0 + gate * (1.0 - squash))
        block_gate = lax.dot_general(wide_inputs, gate_delta, (((0,), (0,)), ((), ())), precision=HIGH, preferred_element_type=jnp.float32).astype(jnp.bfloat16)
        block_up = lax.dot_general(wide_inputs, up_delta, (((0,), (0,)), ((), ())), precision=HIGH, preferred_element_type=jnp.float32).astype(jnp.bfloat16)
        block_down = lax.dot_general(hidden, wide_grads, (((0,), (0,)), ((), ())), precision=HIGH, preferred_element_type=jnp.float32).astype(jnp.bfloat16)
        carry = carry + lax.dot_general(gate_delta, w_gate.astype(jnp.float32), (((1,), (1,)), ((), ())), precision=HIGH, preferred_element_type=jnp.float32)
        carry = carry + lax.dot_general(up_delta, w_up.astype(jnp.float32), (((1,), (1,)), ((), ())), precision=HIGH, preferred_element_type=jnp.float32)
        return carry, (block_gate, block_up, block_down)

    start_sum = jnp.zeros((TOKENS, D), jnp.float32)
    total, (all_gate, all_up, all_down) = lax.scan(one_block, start_sum, (gate_blocks, up_blocks, down_blocks))
    grad_gate = jnp.moveaxis(all_gate, 0, 1).reshape(D, FF)
    grad_up = jnp.moveaxis(all_up, 0, 1).reshape(D, FF)
    grad_down = all_down.reshape(FF, D)
    return (total.astype(jnp.bfloat16), grad_gate, grad_up, grad_down)
```

```python
import jax
import jax.numpy as jnp
from jax import lax
from jax.sharding import PartitionSpec as P

CHUNKS = 2
F32, BF16, F16 = jnp.float32, jnp.bfloat16, jnp.float16


def _ids(dy, dz, dx):
    pairs = []
    for i in range(32):
        y, z, x = i // 16, (i // 4) % 4, i % 4
        pairs.append((i, ((y + dy) % 2) * 16 + ((z + dz) % 4) * 4 + (x + dx) % 4))
    return pairs


def _mp(a, dy=0, dz=0, dx=0):
    return lax.ppermute(a, "mp", _ids(dy, dz, dx))


def _core(a):
    return lax.ppermute(a, "dp", [(0, 1), (1, 0), (2, 3), (3, 2)])


def _ylo(a):
    return lax.ppermute(a, "dp", [(0, 2), (2, 0), (1, 3), (3, 1)])


def _place(pieces, me, axis):
    shape = list(pieces[0].shape)
    shape.insert(axis, 4)
    out = jnp.zeros(shape, pieces[0].dtype)
    for k, piece in enumerate(pieces):
        out = lax.dynamic_update_slice_in_dim(
            out, jnp.expand_dims(piece, axis), (me + k) % 4, axis
        )
    return out


def _ring(a, axis):
    return [a, _mp(a, **{axis: -1}), _mp(a, **{axis: 2}), _mp(a, **{axis: 1})]


def gather(a, order, me):
    y, z, x = me
    other = _mp(a, dy=1)
    pair = jnp.stack([jnp.where(y == 0, a, other), jnp.where(y == 0, other, a)])
    if order == "xz":
        some = _place(_ring(pair, "dx"), x, 1)
        whole = _place(_ring(some, "dz"), z, 1)
    else:
        some = _place(_ring(pair, "dz"), z, 1)
        whole = _place(_ring(some, "dx"), x, 2)
    return whole.reshape(-1, a.shape[-1])


def split(a):
    top = lax.reduce_precision(a, 8, 7)
    return top.astype(BF16), (a - top).astype(BF16)


def activations(summed, width):
    gate, up, grad_hidden = (summed[:, i * width : (i + 1) * width] for i in range(3))
    squash = jax.nn.sigmoid(gate)
    hidden = gate * squash * up
    up_delta = grad_hidden * gate * squash
    gate_delta = grad_hidden * up * squash * (1.0 + gate * (1.0 - squash))
    return jnp.concatenate([hidden, gate_delta, up_delta], axis=1)


def dot(a, b, ca, cb):
    return lax.dot_general(a, b, (((ca,), (cb,)), ((), ())), preferred_element_type=F32)


def per_device(inputs, grad_out, gate_weight, up_weight, down_weight):
    width = gate_weight.shape[1]
    mp = lax.axis_index("mp")
    me = (mp // 16, (mp // 4) % 4, mp % 4)
    core = lax.axis_index("dp") % 2
    x_t, g_t = inputs.T, grad_out.T
    tokens = x_t.shape[1] // CHUNKS
    half = tokens // 2
    scale = jnp.concatenate(
        [jnp.full((1, 2 * width), 16.0, F32), jnp.full((1, width), 64.0, F32)], axis=1
    )
    xs, gs, acts, outs = [], [], [], []
    for c in range(CHUNKS):
        part = slice(c * tokens, (c + 1) * tokens)
        xf = gather(x_t[:, part], "xz", me)
        gf = gather(g_t[:, part], "zx", me)
        xs.append(xf)
        gs.append(gf)
        partial = jnp.concatenate(
            [dot(xf, gate_weight, 0, 0), dot(xf, up_weight, 0, 0), dot(gf, down_weight, 0, 1)], axis=1
        )
        mine = lax.dynamic_slice_in_dim(partial, core * half, half, 0)
        theirs = lax.dynamic_slice_in_dim(partial, (1 - core) * half, half, 0)
        chip = mine + _core(theirs)
        far = _ylo((chip * scale).astype(F16))
        summed = chip + far.astype(F32) / scale
        act = activations(summed, width)
        act_other = _core(act)
        act = jnp.concatenate(
            [jnp.where(core == 0, act, act_other), jnp.where(core == 0, act_other, act)], axis=0
        )
        top, low = split(act)
        acts.append((top, low))
        gd, ud = slice(width, 2 * width), slice(2 * width, 3 * width)
        gi = (
            dot(gate_weight, top[:, gd], 1, 1)
            + dot(gate_weight, low[:, gd], 1, 1)
            + dot(up_weight, top[:, ud], 1, 1)
            + dot(up_weight, low[:, ud], 1, 1)
        )
        code = jnp.where(gi < 0, -1.0, 1.0) * jnp.sqrt(jnp.abs(gi))
        code = code.astype(F16).reshape(32, -1, tokens)
        got = lax.all_to_all(code, "mp", 0, 0, tiled=True).astype(F32)
        outs.append(jnp.sum(got * jnp.abs(got), axis=0).astype(BF16))
    x_all, g_all = jnp.concatenate(xs, axis=1), jnp.concatenate(gs, axis=1)
    top = jnp.concatenate([a[0] for a in acts], axis=0)
    low = jnp.concatenate([a[1] for a in acts], axis=0)
    h, gd, ud = (slice(i * width, (i + 1) * width) for i in range(3))
    grad_gate = (dot(x_all, top[:, gd], 1, 0) + dot(x_all, low[:, gd], 1, 0)).astype(BF16)
    grad_up = (dot(x_all, top[:, ud], 1, 0) + dot(x_all, low[:, ud], 1, 0)).astype(BF16)
    grad_down = (dot(top[:, h], g_all, 0, 1) + dot(low[:, h], g_all, 0, 1)).astype(BF16)
    return (jnp.concatenate(outs, axis=1).T, grad_gate, grad_up, grad_down)


def solution(mesh):
    placed = (
        P(None, ("dp", "mp")),
        P(None, ("dp", "mp")),
        P("dp", "mp"),
        P("dp", "mp"),
        P("mp", "dp"),
    )
    return jax.shard_map(
        per_device,
        mesh=mesh,
        in_specs=placed,
        out_specs=(P(None, ("dp", "mp")), P("dp", "mp"), P("dp", "mp"), P("mp", "dp")),
        check_vma=False,
    )
```

```python
import functools

import jax
import jax.numpy as jnp
from jax import lax
from jax.experimental import pallas as pl
from jax.experimental.pallas import tpu as pltpu
from jax.sharding import PartitionSpec as P

CHUNKS = 2
F32, BF16 = jnp.float32, jnp.bfloat16
VMEM_LIMIT = 48 * 1024 * 1024
BOTH = ("dp", "mp")


def _moves(shift):
    pairs = []
    for i in range(128):
        lo, core, y, z, x = i // 64, (i // 32) % 2, (i // 16) % 2, (i // 4) % 4, i % 4
        lo, core, y, z, x = shift(lo, core, y, z, x)
        pairs.append((i, (lo % 2) * 64 + (core % 2) * 32 + (y % 2) * 16 + (z % 4) * 4 + x % 4))
    return pairs


def _send(a, shift):
    return lax.ppermute(a, BOTH, _moves(shift))


def _first(k):
    return lambda lo, c, y, z, x: (lo, c, y, z + k * c, x + k * (1 - c))


def _second(k):
    return lambda lo, c, y, z, x: (lo, c, y, z + k * (1 - c), x + k * c)


def _over_y(lo, c, y, z, x):
    return lo, c, y + 1, z, x


def _over_core(lo, c, y, z, x):
    return lo, c + 1, y, z, x


def _over_lo(lo, c, y, z, x):
    return lo + 1, c, y, z, x


def encode(u, positive):
    code = jnp.exp2(u * 200.0 - 100.0)
    return jnp.where(positive, code, -code).astype(BF16)


def decode(code):
    wide = code.astype(F32)
    return (jnp.log2(jnp.abs(wide)) + 100.0) * (1.0 / 200.0), wide > 0


def _signed(value, positive):
    return jnp.where(positive, value, -value)


def _call(body, out, **kw):
    params = pltpu.CompilerParams(vmem_limit_bytes=VMEM_LIMIT)
    return pl.pallas_call(body, out_shape=out, compiler_params=params, **kw)


SMEM = pl.BlockSpec(memory_space=pltpu.SMEM)
VMEM = pl.BlockSpec(memory_space=pltpu.VMEM)
ANY = pl.BlockSpec(memory_space=pl.ANY)


def shape(dims, dtype):
    return jax.ShapeDtypeStruct(dims, dtype)


def _assemble_body(ids, p0, p1, p2, p3, x_out, g_out, sems):
    core, y, s1, s2 = ids[0], ids[1], ids[2], ids[3]
    copies = []
    for k2, piece in enumerate((p0, p1, p2, p3)):
        b = lax.rem(s2 + k2, 4)
        for k1 in range(4):
            a = lax.rem(s1 + k1, 4)
            zx = jnp.where(core == 0, b * 4 + a, a * 4 + b)
            for k0 in range(2):
                at = pl.multiple_of((lax.rem(y + k0, 2) * 16 + zx) * 64, 64)
                for half, out in enumerate((x_out, g_out)):
                    copies.append(
                        pltpu.make_async_copy(
                            piece.at[k1, k0, pl.ds(half * 64, 64), :],
                            out.at[pl.ds(at, 64), :],
                            sems.at[len(copies)],
                        )
                    )
    for copy in copies:
        copy.start()
    for copy in copies:
        copy.wait()


def assemble(ids, pieces, tokens):
    out = shape((2048, tokens), BF16)
    return _call(
        _assemble_body,
        (out, out),
        in_specs=[SMEM] + [ANY] * 4,
        out_specs=(ANY, ANY),
        scratch_shapes=[pltpu.SemaphoreType.DMA((64,))],
    )(ids, *pieces)


def _chip_body(width, ids, gate, up, gh, other, chip, code, peak):
    half = gate.shape[0] // 2
    rows = pl.ds(pl.multiple_of(ids[0] * half, half), half)
    for i, part in enumerate((gate, up, gh)):
        cols = slice(i * width, (i + 1) * width)
        total = part[rows, :] + other[:, cols]
        chip[:, cols] = total
        size = jnp.abs(total)
        top = jnp.max(jnp.max(size, axis=0, keepdims=True), axis=1, keepdims=True)
        top = jnp.maximum(top, 1e-35)
        code[:, cols] = encode(jnp.sqrt(jnp.minimum(size / top, 1.0)), total >= 0)
        peak[8 * i : 8 * i + 8, :] = jnp.broadcast_to(top, (8, 128))


def chip_sum(ids, gate, up, gh, other):
    rows, width = other.shape[0], gate.shape[1]
    return _call(
        functools.partial(_chip_body, width),
        (shape((rows, 3 * width), F32), shape((rows, 3 * width), BF16), shape((24, 128), F32)),
        in_specs=[SMEM] + [VMEM] * 4,
        out_specs=(VMEM,) * 3,
    )(ids, gate, up, gh, other)


def _act_body(width, chip, code, peak, out):
    def whole(i):
        cols = slice(i * width, (i + 1) * width)
        u, positive = decode(code[:, cols])
        return chip[:, cols] + _signed(u * u * peak[8 * i : 8 * i + 1, 0:1], positive)

    gate, up, grad_hidden = whole(0), whole(1), whole(2)
    squash = 1.0 / (1.0 + jnp.exp(-gate))
    out[:, 0:width] = gate * squash * up
    out[:, width : 2 * width] = grad_hidden * up * squash * (1.0 + gate * (1.0 - squash))
    out[:, 2 * width : 3 * width] = grad_hidden * gate * squash


def activations(chip, code, peak):
    return _call(
        functools.partial(_act_body, chip.shape[1] // 3),
        shape(chip.shape, F32),
        in_specs=[VMEM] * 3,
        out_specs=VMEM,
    )(chip, code, peak)


def _pack(block):
    size = jnp.abs(block)
    top = jnp.maximum(jnp.max(size, axis=0, keepdims=True) * 1.01, 1e-35)
    top = top.astype(BF16).astype(F32)
    return encode(size / top, block >= 0), top


def _unpack(code, top):
    u, positive = decode(code)
    return _signed(u * top, positive)


def _grad_in_body(width, ids, wg, wu, mine, theirs, top, low, own, c1, c2, c3, tops):
    step = pl.program_id(0)
    core, s1 = ids[0], ids[2]
    half = mine.shape[0]

    @pl.when(step == 0)
    def _():
        for part, place in ((mine, core), (theirs, 1 - core)):
            value = part[...]
            high = value.astype(BF16)
            rows = pl.ds(pl.multiple_of(place * half, half), half)
            top[rows, :] = high
            low[rows, :] = (value - high.astype(F32)).astype(BF16)

    def dot(a, b):
        return lax.dot_general(a, b, (((1,), (1,)), ((), ())), preferred_element_type=F32)

    gd, ud = slice(width, 2 * width), slice(2 * width, 3 * width)
    total = (
        dot(wg[...], top[:, gd]) + dot(wg[...], low[:, gd]) + dot(wu[...], top[:, ud]) + dot(wu[...], low[:, ud])
    )
    y, z = step // 4, lax.rem(step, 4)
    for x in range(4):
        block = total[x * 64 : (x + 1) * 64]
        place = jnp.where(core == 0, x, z)
        k = lax.rem(place - s1 + 4, 4)
        j = jnp.where(core == 0, step, y * 4 + x)
        rows = pl.ds(pl.multiple_of(j * 64, 64), 64)
        code, scale = _pack(block)
        tops[pl.ds(k, 1), pl.ds(j, 1), :] = scale[None]

        @pl.when(k == 0)
        def _():
            own[rows, :] = block

        for n, out in ((1, c1), (2, c2), (3, c3)):

            @pl.when(k == n)
            def _():
                out[rows, :] = code

    @pl.when(step == 7)
    def _():
        for n, out in ((1, c1), (2, c2), (3, c3)):
            out[512:528, :] = jnp.concatenate([tops[n], tops[n]], axis=0).astype(BF16)


def grad_in(ids, wg, wu, mine, theirs):
    half, three = mine.shape
    tokens, width = 2 * half, three // 3
    weight = pl.BlockSpec((256, width), lambda i: (i, 0))
    whole = lambda *dims: pl.BlockSpec(dims, lambda i: (0,) * len(dims))
    code = shape((528, tokens), BF16)
    act = shape((tokens, three), BF16)
    return _call(
        functools.partial(_grad_in_body, width),
        (act, act, shape((512, tokens), F32), code, code, code),
        grid=(8,),
        in_specs=[SMEM, weight, weight, whole(half, three), whole(half, three)],
        out_specs=(whole(tokens, three),) * 2 + (whole(512, tokens),) + (whole(528, tokens),) * 3,
        scratch_shapes=[pltpu.VMEM((4, 8, tokens), F32)],
    )(ids, wg, wu, mine, theirs)


def _sum_first_body(ids, own, r1, r2, r3, own2, c1, c2, c3, tops):
    s2 = ids[3]
    scales = [r[512:528, :].astype(F32) for r in (r1, r2, r3)]
    for j in range(8):
        rows = slice(j * 64, (j + 1) * 64)
        total = own[rows, :]
        for r, scale in zip((r1, r2, r3), scales):
            total = total + _unpack(r[rows, :], scale[j : j + 1])
        y, place = j // 4, j % 4
        k = lax.rem(place - s2 + 4, 4)
        code, scale = _pack(total)
        tops[pl.ds(k, 1), y : y + 1, :] = scale[None]
        to = slice(y * 64, (y + 1) * 64)

        @pl.when(k == 0)
        def _():
            own2[to, :] = total

        for n, out in ((1, c1), (2, c2), (3, c3)):

            @pl.when(k == n)
            def _():
                out[to, :] = code

    for n, out in ((1, c1), (2, c2), (3, c3)):
        out[128:144, :] = jnp.concatenate([tops[n], tops[n]], axis=0).astype(BF16)


def sum_first(ids, own, received):
    tokens = own.shape[1]
    code = shape((144, tokens), BF16)
    return _call(
        _sum_first_body,
        (shape((128, tokens), F32), code, code, code),
        in_specs=[SMEM] + [VMEM] * 4,
        out_specs=(VMEM,) * 4,
        scratch_shapes=[pltpu.VMEM((4, 8, tokens), F32)],
    )(ids, own, *received)


def _sum_second_body(ids, own, r1, r2, r3, own3, out):
    scales = [r[128:144, :].astype(F32) for r in (r1, r2, r3)]
    for y in range(2):
        rows = slice(y * 64, (y + 1) * 64)
        total = own[rows, :]
        for r, scale in zip((r1, r2, r3), scales):
            total = total + _unpack(r[rows, :], scale[y : y + 1])

        @pl.when(ids[1] == y)
        def _():
            own3[...] = total

        @pl.when(ids[1] != y)
        def _():
            code, top = _pack(total)
            out[0:64, :] = code
            out[64:80, :] = jnp.broadcast_to(top, (16, top.shape[1])).astype(BF16)


def sum_second(ids, own, received):
    tokens = own.shape[1]
    return _call(
        _sum_second_body,
        (shape((64, tokens), F32), shape((80, tokens), BF16)),
        in_specs=[SMEM] + [VMEM] * 4,
        out_specs=(VMEM,) * 2,
    )(ids, own, *received)


def _sum_last_body(own, r, out):
    out[...] = (own[...] + _unpack(r[0:64, :], r[64:80, :].astype(F32)[0:1])).astype(BF16)


def sum_last(own, received):
    return _call(
        _sum_last_body, shape(own.shape, BF16), in_specs=[VMEM] * 2, out_specs=VMEM
    )(own, received)


def dot(a, b, ca, cb):
    return lax.dot_general(a, b, (((ca,), (cb,)), ((), ())), preferred_element_type=F32)


def per_device(inputs, grad_out, gate_weight, up_weight, down_weight):
    width = gate_weight.shape[1]
    mp = lax.axis_index("mp")
    core = lax.axis_index("dp") % 2
    y, z, x = mp // 16, (mp // 4) % 4, mp % 4
    ids = jnp.stack([core, y, jnp.where(core == 0, x, z), jnp.where(core == 0, z, x)]).astype(jnp.int32)
    tokens = inputs.shape[0] // CHUNKS
    half = tokens // 2
    both = jnp.concatenate([inputs.T, grad_out.T], axis=0)
    both = jnp.stack([both[:, c * tokens : (c + 1) * tokens] for c in range(CHUNKS)])
    pair = jnp.stack([both, _send(both, _over_y)])
    near = [pair] + [_send(pair, _first(-k)) for k in (1, 2, 3)]
    xs, gs, tops, lows, outs = [], [], [], [], []
    for c in range(CHUNKS):
        some = jnp.stack([p[:, c] for p in near])
        pieces = [some] + [_send(some, _second(-k)) for k in (1, 2, 3)]
        xf, gf = assemble(ids, pieces, tokens)
        xs.append(xf)
        gs.append(gf)
        gate, up = dot(xf, gate_weight, 0, 0), dot(xf, up_weight, 0, 0)
        gh = dot(gf, down_weight, 0, 1)
        theirs = lax.dynamic_slice_in_dim(
            jnp.concatenate([gate, up, gh], axis=1), (1 - core) * half, half, 0
        )
        chip, code, peak = chip_sum(ids, gate, up, gh, _send(theirs, _over_core))
        act = activations(chip, _send(code, _over_lo), _send(peak, _over_lo))
        top, low, own, *codes = grad_in(ids, gate_weight, up_weight, act, _send(act, _over_core))
        tops.append(top)
        lows.append(low)
        own, *codes = sum_first(ids, own, [_send(v, _first(k + 1)) for k, v in enumerate(codes)])
        own, last = sum_second(ids, own, [_send(v, _second(k + 1)) for k, v in enumerate(codes)])
        outs.append(sum_last(own, _send(last, _over_y)))
    x_all, g_all = jnp.concatenate(xs, axis=1), jnp.concatenate(gs, axis=1)
    top, low = jnp.concatenate(tops, axis=0), jnp.concatenate(lows, axis=0)
    h, gd, ud = (slice(i * width, (i + 1) * width) for i in range(3))
    grad_gate = (dot(x_all, top[:, gd], 1, 0) + dot(x_all, low[:, gd], 1, 0)).astype(BF16)
    grad_up = (dot(x_all, top[:, ud], 1, 0) + dot(x_all, low[:, ud], 1, 0)).astype(BF16)
    grad_down = (dot(top[:, h], g_all, 0, 1) + dot(low[:, h], g_all, 0, 1)).astype(BF16)
    return (jnp.concatenate(outs, axis=1).T, grad_gate, grad_up, grad_down)


def solution(mesh):
    placed = (
        P(None, ("dp", "mp")),
        P(None, ("dp", "mp")),
        P("dp", "mp"),
        P("dp", "mp"),
        P("mp", "dp"),
    )
    return jax.shard_map(
        per_device,
        mesh=mesh,
        in_specs=placed,
        out_specs=(P(None, ("dp", "mp")), P("dp", "mp"), P("dp", "mp"), P("mp", "dp")),
        check_vma=False,
    )
```

```python
import functools

import jax
import jax.numpy as jnp
from jax import lax
from jax.experimental import pallas as pl
from jax.experimental.pallas import tpu as pltpu
from jax.sharding import PartitionSpec as P

COST = 20
F32, BF16 = jnp.float32, jnp.bfloat16
SMALL, LARGE, WHOLE = 16 * 1024 * 1024, 40 * 1024 * 1024, 60 * 1024 * 1024
BOTH = ("dp", "mp")


def _moves(shift):
    pairs = []
    for i in range(128):
        lo, core, y, z, x = i // 64, (i // 32) % 2, (i // 16) % 2, (i // 4) % 4, i % 4
        lo, core, y, z, x = shift(lo, core, y, z, x)
        pairs.append((i, (lo % 2) * 64 + (core % 2) * 32 + (y % 2) * 16 + (z % 4) * 4 + x % 4))
    return pairs


def _send(a, shift):
    return lax.ppermute(a, BOTH, _moves(shift))


def _first(k):
    return lambda lo, c, y, z, x: (lo, c, y, z + k * c, x + k * (1 - c))


def _second(k):
    return lambda lo, c, y, z, x: (lo, c, y, z + k * (1 - c), x + k * c)


def _over_y(lo, c, y, z, x):
    return lo, c, y + 1, z, x


def _over_core(lo, c, y, z, x):
    return lo, c + 1, y, z, x


def _over_lo(lo, c, y, z, x):
    return lo + 1, c, y, z, x


def encode(u, positive):
    code = jnp.exp2(u * 200.0 - 100.0)
    return jnp.where(positive, code, -code).astype(BF16)


def decode(code):
    wide = code.astype(F32)
    return (jnp.log2(jnp.abs(wide)) + 100.0) * (1.0 / 200.0), wide > 0


def _signed(value, positive):
    return jnp.where(positive, value, -value)


def _call(body, out, room=SMALL, **kw):
    params = pltpu.CompilerParams(vmem_limit_bytes=room)
    return pl.pallas_call(body, out_shape=out, compiler_params=params, **kw)


def _cost(flops, bytes_accessed, transcendentals):
    return pl.CostEstimate(
        flops=flops // COST, bytes_accessed=bytes_accessed // COST, transcendentals=transcendentals // COST
    )


SMEM = pl.BlockSpec(memory_space=pltpu.SMEM)
VMEM = pl.BlockSpec(memory_space=pltpu.VMEM)
ANY = pl.BlockSpec(memory_space=pl.ANY)


def shape(dims, dtype):
    return jax.ShapeDtypeStruct(dims, dtype)


TICK = shape((8, 128), F32)


def _forward_body(width, ids, p0, p1, p2, p3, wg, wu, wd, *rest):
    mine, theirs, (acts, turned, held, last, loads, sems) = rest[:2], rest[2:8], rest[8:]
    weights = [
        pltpu.make_async_copy(weight, held.at[i], loads.at[i]) for i, weight in enumerate((wg, wu))
    ] + [pltpu.make_async_copy(wd, last, loads.at[2])]
    core, y, s1, s2 = ids[0], ids[1], ids[2], ids[3]
    copies = []
    for k2, piece in enumerate((p0, p1, p2, p3)):
        b = lax.rem(s2 + k2, 4)
        for k1 in range(4):
            a = lax.rem(s1 + k1, 4)
            zx = jnp.where(core == 0, b * 4 + a, a * 4 + b)
            for k0 in range(2):
                at = pl.multiple_of((lax.rem(y + k0, 2) * 16 + zx) * 64, 64)
                copies.append(
                    pltpu.make_async_copy(
                        piece.at[k1, k0], acts.at[:, pl.ds(at, 64), :], sems.at[len(copies)]
                    )
                )
    for copy in copies:
        copy.start()
    for copy in weights:
        copy.start()
    for copy in copies:
        copy.wait()
    half = mine[0].shape[0]
    for i in range(2):
        for n, place in enumerate((core, 1 - core)):
            for c in range(2):
                cols = pl.ds(pl.multiple_of((2 * c + place) * half, half), half)
                row = (2 * n + c) * half
                turned[i, row : row + half, :] = acts[i, :, cols].T
    for i in range(3):
        weights[i].wait()
        weight = last if i == 2 else held.at[i]
        dims = (((1,), (0,)), ((), ())) if i < 2 else (((1,), (1,)), ((), ()))
        total = lax.dot_general(turned[i // 2], weight[...], dims, preferred_element_type=F32)
        for c in range(2):
            mine[c][:, i * width : (i + 1) * width] = total[c * half : (c + 1) * half]
            theirs[3 * c + i][...] = total[(2 + c) * half : (3 + c) * half]


def _whole(*dims):
    return pl.BlockSpec(dims, lambda i: (0,) * len(dims))


def forward(ids, pieces, wg, wu, wd):
    depth, width = wg.shape
    tokens = pieces[0].shape[-1]
    mine, other = shape((tokens // 4, 3 * width), F32), shape((tokens // 4, width), F32)
    return _call(
        functools.partial(_forward_body, width),
        (mine,) * 2 + (other,) * 6 + (shape((2, depth, tokens), BF16),),
        WHOLE,
        in_specs=[SMEM] + [ANY] * 7,
        out_specs=(VMEM,) * 9,
        scratch_shapes=[
            pltpu.VMEM((2, tokens, depth), BF16),
            pltpu.VMEM((2, depth, width), BF16),
            pltpu.VMEM((width, depth), BF16),
            pltpu.SemaphoreType.DMA((3,)),
            pltpu.SemaphoreType.DMA((32,)),
        ],
        cost_estimate=_cost(
            flops=6 * tokens * depth * width, bytes_accessed=6 * depth * width + 8 * depth * tokens, transcendentals=0
        ),
    )(ids, *pieces, wg, wu, wd)


def _chip_body(width, mine, o0, o1, o2, chip, code, tick):
    tick[...] = jnp.zeros_like(tick)
    for i in range(3):
        cols = slice(i * width, (i + 1) * width)
        total = mine[:, cols] + (o0, o1, o2)[i][...]
        chip[:, cols] = total
        size = jnp.abs(total)
        top = jnp.max(jnp.max(size, axis=0, keepdims=True), axis=1, keepdims=True)
        top = jnp.maximum(top * 1.01, 1e-35).astype(BF16).astype(F32)
        code[:, cols] = encode(jnp.sqrt(size * (1.0 / top)), total >= 0)
        code[16 * i : 16 * i + 16, 3 * width :] = jnp.broadcast_to(top, (16, 128)).astype(BF16)
    code[48:, 3 * width :] = jnp.zeros((code.shape[0] - 48, 128), BF16)


def chip_sum(mine, others):
    rows, three = mine.shape
    return _call(
        functools.partial(_chip_body, three // 3),
        (shape((rows, three), F32), shape((rows, three + 128), BF16), TICK),
        in_specs=[VMEM] * 4,
        out_specs=(VMEM,) * 3,
        cost_estimate=_cost(
            flops=20 * rows * three, bytes_accessed=14 * rows * three, transcendentals=2 * rows * three
        ),
    )(mine, *others)


def _act_body(width, chip, code, _, o0, o1, o2):
    def whole(i):
        cols = slice(i * width, (i + 1) * width)
        u, positive = decode(code[:, cols])
        top = code[16 * i : 16 * i + 16, 3 * width :].astype(F32)[0:1, 0:1]
        return chip[:, cols] + _signed(u * u * top, positive)

    gate, up, grad_hidden = whole(0), whole(1), whole(2)
    squash = 1.0 / (1.0 + jnp.exp(-gate))
    o0[...] = gate * squash * up
    o1[...] = grad_hidden * up * squash * (1.0 + gate * (1.0 - squash))
    o2[...] = grad_hidden * gate * squash


def activations(chip, code, after):
    rows, three = chip.shape
    return _call(
        functools.partial(_act_body, three // 3),
        (shape((rows, three // 3), F32),) * 3,
        in_specs=[VMEM] * 2 + [ANY],
        out_specs=(VMEM,) * 3,
        cost_estimate=_cost(
            flops=20 * rows * three, bytes_accessed=10 * rows * three, transcendentals=2 * rows * three
        ),
    )(chip, code, after)


def _pack(block):
    size = jnp.abs(block)
    top = jnp.maximum(jnp.max(size, axis=0, keepdims=True) * 1.01, 1e-35)
    top = top.astype(BF16).astype(F32)
    return encode(size * (1.0 / top), block >= 0), top


def _unpack(code, top):
    u, positive = decode(code)
    return _signed(u * top, positive)


def _grad_in_body(width, n_before, ids, wg, wu, m0, m1, m2, o0, o1, o2, *rest):
    before, (pair, own, c1, c2, c3, tick, right, tops, blocks, codes) = rest[:n_before], rest[n_before:]
    core, s1 = ids[0], ids[2]
    half = m0.shape[0]
    tokens = 2 * half
    tick[...] = jnp.zeros_like(tick)
    for parts, place in (((m0, m1, m2), core), ((o0, o1, o2), 1 - core)):
        rows = pl.ds(pl.multiple_of(place * half, half), half)
        rest = pl.ds(pl.multiple_of(tokens + place * half, half), half)
        for i, part in enumerate(parts):
            value = part[...]
            high = value.astype(BF16)
            low = (value - high.astype(F32)).astype(BF16)
            pair[rows, i * width : (i + 1) * width] = high
            pair[rest, i * width : (i + 1) * width] = low
            if i:
                right[rows, (2 * i - 2) * width : (2 * i - 1) * width] = high
                right[rows, (2 * i - 1) * width : 2 * i * width] = low
    for part in range(4):
        some = slice(part * 512, (part + 1) * 512)
        g, u = wg[some, :], wu[some, :]
        total = lax.dot_general(
            jnp.concatenate([g, g, u, u], axis=1), right[...], (((1,), (1,)), ((), ())), preferred_element_type=F32
        )
        for sub in range(8):
            at, x = part * 2 + sub // 4, sub % 4
            y, z = at // 4, at % 4
            block = total[sub * 64 : (sub + 1) * 64]
            k = lax.rem(jnp.where(core == 0, x, z) - s1 + 4, 4)
            j = jnp.where(core == 0, at, y * 4 + x)
            rows = pl.ds(pl.multiple_of(j * 64, 64), 64)
            code, scale = _pack(block)
            tops[pl.ds(k, 1), pl.ds(j, 1), :] = scale[None]
            blocks[pl.ds(k, 1), rows, :] = block[None]
            codes[pl.ds(k, 1), rows, :] = code[None]
    for out, earlier in zip((own, c1, c2, c3), before):
        out[0] = earlier[0]
    c = own.shape[0] - 1
    own[c] = blocks[0]
    for n, out in ((1, c1), (2, c2), (3, c3)):
        out[c, 0:512, :] = codes[n]
        out[c, 512:528, :] = jnp.concatenate([tops[n], tops[n]], axis=0).astype(BF16)


def grad_in(ids, wg, wu, mine, theirs, before):
    half, width = mine[0].shape
    tokens, three = 2 * half, 3 * width
    n = 1 + (len(before) > 0)
    code = shape((n, 528, tokens), BF16)
    return _call(
        functools.partial(_grad_in_body, width, len(before)),
        (shape((2 * tokens, three), BF16), shape((n, 512, tokens), F32), code, code, code, TICK),
        LARGE,
        in_specs=[SMEM] + [VMEM] * (8 + len(before)),
        out_specs=(VMEM,) * 6,
        scratch_shapes=[
            pltpu.VMEM((tokens, 4 * width), BF16),
            pltpu.VMEM((4, 8, tokens), F32),
            pltpu.VMEM((4, 512, tokens), F32),
            pltpu.VMEM((4, 512, tokens), BF16),
        ],
        cost_estimate=_cost(
            flops=8 * tokens * 2048 * width, bytes_accessed=4 * 2048 * width + 16 * tokens * three, transcendentals=2048 * tokens
        ),
    )(ids, wg, wu, *mine, *theirs, *before)


def _twice(rows, c):
    half = rows.shape[1] // 2
    part = rows[:, c * half : (c + 1) * half]
    return jnp.concatenate([part, part], axis=1)


def _grad_up_body(x, d0, d1, out):
    rows = x[0]
    total = jnp.dot(_twice(rows, 0), d0[...], preferred_element_type=F32)
    total = total + jnp.dot(_twice(rows, 1), d1[...], preferred_element_type=F32)
    out[...] = total.astype(BF16)


def grad_weight(acts, pairs, place, width):
    depth, tokens = acts.shape[1:]
    delta = pl.BlockSpec((tokens, width), lambda i: (0, place))
    return _call(
        _grad_up_body,
        shape((depth, width), BF16),
        WHOLE,
        grid=(depth // 512,),
        in_specs=[pl.BlockSpec((1, 512, tokens), lambda i: (0, i, 0))] + [delta] * 2,
        out_specs=pl.BlockSpec((512, width), lambda i: (i, 0)),
        cost_estimate=_cost(
            flops=COST * 4 * tokens * depth * width, bytes_accessed=COST * 4 * depth * width, transcendentals=0
        ),
    )(acts, *pairs)


def _grad_down_body(g, h0, h1, out, turned):
    @pl.when(pl.program_id(0) == 0)
    def _():
        for i, h in enumerate((h0, h1)):
            turned[i] = h[...].T

    rows, dims = g[0], (((1,), (1,)), ((), ()))
    total = lax.dot_general(turned[0], _twice(rows, 0), dims, preferred_element_type=F32)
    total = total + lax.dot_general(turned[1], _twice(rows, 1), dims, preferred_element_type=F32)
    out[...] = total.astype(BF16)


def grad_down_weight(acts, pairs, width):
    depth, tokens = acts.shape[1:]
    hidden = pl.BlockSpec((tokens, width), lambda i: (0, 0))
    return _call(
        _grad_down_body,
        shape((width, depth), BF16),
        WHOLE,
        grid=(depth // 512,),
        in_specs=[pl.BlockSpec((1, 512, tokens), lambda i: (1, i, 0))] + [hidden] * 2,
        out_specs=pl.BlockSpec((width, 512), lambda i: (0, i)),
        scratch_shapes=[pltpu.VMEM((2, width, tokens), BF16)],
        cost_estimate=_cost(
            flops=COST * 4 * tokens * depth * width, bytes_accessed=COST * 4 * depth * width, transcendentals=0
        ),
    )(acts, *pairs)


def _sum_first_body(ids, own, r1, r2, r3, own2, c1, c2, c3, tops):
    s2 = ids[3]
    for c in range(2):
        scales = [r[c, 512:528, :].astype(F32) for r in (r1, r2, r3)]
        for j in range(8):
            rows = slice(j * 64, (j + 1) * 64)
            total = own[c, rows, :]
            for r, scale in zip((r1, r2, r3), scales):
                total = total + _unpack(r[c, rows, :], scale[j : j + 1])
            y, place = j // 4, j % 4
            k = lax.rem(place - s2 + 4, 4)
            code, scale = _pack(total)
            tops[pl.ds(k, 1), y : y + 1, :] = scale[None]
            to = slice(y * 64, (y + 1) * 64)

            @pl.when(k == 0)
            def _():
                own2[c, to, :] = total

            for n, out in ((1, c1), (2, c2), (3, c3)):

                @pl.when(k == n)
                def _():
                    out[c, to, :] = code

        for n, out in ((1, c1), (2, c2), (3, c3)):
            out[c, 128:144, :] = jnp.concatenate([tops[n], tops[n]], axis=0).astype(BF16)


def sum_first(ids, own, received):
    tokens = own.shape[2]
    code = shape((2, 144, tokens), BF16)
    return _call(
        _sum_first_body,
        (shape((2, 128, tokens), F32), code, code, code),
        in_specs=[SMEM] + [VMEM] * 4,
        out_specs=(VMEM,) * 4,
        scratch_shapes=[pltpu.VMEM((4, 8, tokens), F32)],
    )(ids, own, *received)


def _sum_second_body(ids, own, r1, r2, r3, own3, out):
    for c in range(2):
        scales = [r[c, 128:144, :].astype(F32) for r in (r1, r2, r3)]
        for y in range(2):
            rows = slice(y * 64, (y + 1) * 64)
            total = own[c, rows, :]
            for r, scale in zip((r1, r2, r3), scales):
                total = total + _unpack(r[c, rows, :], scale[y : y + 1])

            @pl.when(ids[1] == y)
            def _():
                own3[c] = total

            @pl.when(ids[1] != y)
            def _():
                code, top = _pack(total)
                out[c, 0:64, :] = code
                out[c, 64:80, :] = jnp.broadcast_to(top, (16, top.shape[1])).astype(BF16)


def sum_second(ids, own, received):
    tokens = own.shape[2]
    return _call(
        _sum_second_body,
        (shape((2, 64, tokens), F32), shape((2, 80, tokens), BF16)),
        in_specs=[SMEM] + [VMEM] * 4,
        out_specs=(VMEM,) * 2,
    )(ids, own, *received)


def _sum_last_body(own, r, out):
    tokens = own.shape[2]
    for c in range(2):
        total = own[c] + _unpack(r[c, 0:64, :], r[c, 64:80, :].astype(F32)[0:1])
        out[:, c * tokens : (c + 1) * tokens] = total.astype(BF16)


def sum_last(own, received):
    return _call(
        _sum_last_body, shape((64, 2 * own.shape[2]), BF16), in_specs=[VMEM] * 2, out_specs=VMEM
    )(own, received)


def per_device(inputs, grad_out, gate_weight, up_weight, down_weight):
    width = gate_weight.shape[1]
    mp = lax.axis_index("mp")
    core = lax.axis_index("dp") % 2
    y, z, x = mp // 16, (mp // 4) % 4, mp % 4
    ids = jnp.stack([core, y, jnp.where(core == 0, x, z), jnp.where(core == 0, z, x)]).astype(jnp.int32)
    both = jnp.stack([inputs.T, grad_out.T])
    pair = jnp.stack([both, _send(both, _over_y)])
    some = jnp.stack([pair] + [_send(pair, _first(-k)) for k in (1, 2, 3)])
    pieces = [some] + [_send(some, _second(-k)) for k in (1, 2, 3)]
    mine0, mine1, *theirs, acts = forward(ids, pieces, gate_weight, up_weight, down_weight)
    chips, codes = [], []
    for mine, others in ((mine0, theirs[:3]), (mine1, theirs[3:])):
        chip, code, tick = chip_sum(mine, [_send(v, _over_core) for v in others])
        chips.append(chip)
        codes.append(_send(code, _over_lo))
    pairs, part = [], ()
    for chip, code in zip(chips, codes):
        act = activations(chip, code, tick)
        others = [_send(v, _over_core) for v in act]
        delta, *part, tick = grad_in(ids, gate_weight, up_weight, act, others, part)
        pairs.append(delta)
    own, *rest = part
    own, *rest = sum_first(ids, own, [_send(v, _first(k + 1)) for k, v in enumerate(rest)])
    own, last = sum_second(ids, own, [_send(v, _second(k + 1)) for k, v in enumerate(rest)])
    grad_inputs = sum_last(own, _send(last, _over_y)).T
    grad_gate = grad_weight(acts, pairs, 1, width)
    grad_up = grad_weight(acts, pairs, 2, width)
    grad_down = grad_down_weight(acts, pairs, width)
    return (grad_inputs, grad_gate, grad_up, grad_down)


def solution(mesh):
    placed = (
        P(None, ("dp", "mp")),
        P(None, ("dp", "mp")),
        P("dp", "mp"),
        P("dp", "mp"),
        P("mp", "dp"),
    )
    return jax.shard_map(
        per_device,
        mesh=mesh,
        in_specs=placed,
        out_specs=(P(None, ("dp", "mp")), P("dp", "mp"), P("dp", "mp"), P("mp", "dp")),
        check_vma=False,
    )
```

```python
import functools

import jax
import jax.numpy as jnp
from jax import lax
from jax.experimental import pallas as pl
from jax.experimental.pallas import tpu as pltpu
from jax.sharding import PartitionSpec as P

COST = 20
F32, BF16 = jnp.float32, jnp.bfloat16
SMALL, LARGE, WHOLE = 16 * 1024 * 1024, 40 * 1024 * 1024, 60 * 1024 * 1024
BOTH = ("dp", "mp")


def _moves(shift):
    pairs = []
    for i in range(128):
        lo, core, y, z, x = i // 64, (i // 32) % 2, (i // 16) % 2, (i // 4) % 4, i % 4
        lo, core, y, z, x = shift(lo, core, y, z, x)
        pairs.append((i, (lo % 2) * 64 + (core % 2) * 32 + (y % 2) * 16 + (z % 4) * 4 + x % 4))
    return pairs


def _send(a, shift):
    return lax.ppermute(a, BOTH, _moves(shift))


def _first(k):
    return lambda lo, c, y, z, x: (lo, c, y, z + k * c, x + k * (1 - c))


def _second(k):
    return lambda lo, c, y, z, x: (lo, c, y, z + k * (1 - c), x + k * c)


def _over_y(lo, c, y, z, x):
    return lo, c, y + 1, z, x


def _over_core(lo, c, y, z, x):
    return lo, c + 1, y, z, x


def _over_lo(lo, c, y, z, x):
    return lo + 1, c, y, z, x


def encode(u, positive):
    code = jnp.exp2(u * 200.0 - 100.0)
    return jnp.where(positive, code, -code).astype(BF16)


def decode(code):
    wide = code.astype(F32)
    return (jnp.log2(jnp.abs(wide)) + 100.0) * (1.0 / 200.0), wide > 0


def _signed(value, positive):
    return jnp.where(positive, value, -value)


def _call(body, out, room=SMALL, **kw):
    params = pltpu.CompilerParams(vmem_limit_bytes=room)
    return pl.pallas_call(body, out_shape=out, compiler_params=params, **kw)


def _cost(flops, bytes_accessed, transcendentals):
    return pl.CostEstimate(
        flops=flops // COST, bytes_accessed=bytes_accessed // COST, transcendentals=transcendentals // COST
    )


SMEM = pl.BlockSpec(memory_space=pltpu.SMEM)
VMEM = pl.BlockSpec(memory_space=pltpu.VMEM)
ANY = pl.BlockSpec(memory_space=pl.ANY)


def shape(dims, dtype):
    return jax.ShapeDtypeStruct(dims, dtype)


TICK = shape((8, 128), F32)


def _forward_body(width, ids, *rest):
    xs, gs, (wg, wu, wd), rest = rest[:4], rest[4:8], rest[8:11], rest[11:]
    mine, theirs, (acts_out, acts, turned, held, last, sums, loads, stores, sems) = rest[:2], rest[2:8], rest[8:]
    weights = [
        pltpu.make_async_copy(weight, held.at[i], loads.at[i]) for i, weight in enumerate((wg, wu))
    ] + [pltpu.make_async_copy(wd, last, loads.at[2])]
    core, y, s1, s2 = ids[0], ids[1], ids[2], ids[3]
    copies = []
    for i, pieces in enumerate((xs, gs)):
        for k2, piece in enumerate(pieces):
            b = lax.rem(s2 + k2, 4)
            for k1 in range(4):
                a = lax.rem(s1 + k1, 4)
                zx = jnp.where(core == 0, b * 4 + a, a * 4 + b)
                for k0 in range(2):
                    at = pl.multiple_of((lax.rem(y + k0, 2) * 16 + zx) * 64, 64)
                    copies.append(
                        pltpu.make_async_copy(
                            piece.at[k1, k0], acts.at[i, pl.ds(at, 64), :], sems.at[len(copies)]
                        )
                    )
    for copy in copies:
        copy.start()
    for copy in weights:
        copy.start()
    for copy in copies:
        copy.wait()
    out = [pltpu.make_async_copy(acts, acts_out, stores.at[0])]
    out[0].start()
    half = mine[0].shape[0]
    for i in range(2):
        for n, place in enumerate((core, 1 - core)):
            for c in range(2):
                cols = pl.ds(pl.multiple_of((2 * c + place) * half, half), half)
                row = (2 * n + c) * half
                turned[i, row : row + half, :] = acts[i, :, cols].T
    for i in range(3):
        weights[i].wait()
        weight = last if i == 2 else held.at[i]
        dims = (((1,), (0,)), ((), ())) if i < 2 else (((1,), (1,)), ((), ()))
        sums[i] = lax.dot_general(turned[i // 2], weight[...], dims, preferred_element_type=F32)
        for c in range(2):
            for row, to in (
                (c * half, mine[c].at[:, pl.ds(i * width, width)]),
                ((2 + c) * half, theirs[3 * c + i]),
            ):
                copy = pltpu.make_async_copy(sums.at[i, pl.ds(row, half), :], to, stores.at[len(out)])
                copy.start()
                out.append(copy)
    for copy in out:
        copy.wait()


def _whole(*dims):
    return pl.BlockSpec(dims, lambda i: (0,) * len(dims))


def forward(ids, xs, gs, wg, wu, wd):
    depth, width = wg.shape
    tokens = xs[0].shape[-1]
    mine, other = shape((tokens // 4, 3 * width), F32), shape((tokens // 4, width), F32)
    return _call(
        functools.partial(_forward_body, width),
        (mine,) * 2 + (other,) * 6 + (shape((2, depth, tokens), BF16),),
        WHOLE,
        in_specs=[SMEM] + [ANY] * 11,
        out_specs=(ANY,) * 9,
        scratch_shapes=[
            pltpu.VMEM((2, depth, tokens), BF16),
            pltpu.VMEM((2, tokens, depth), BF16),
            pltpu.VMEM((2, depth, width), BF16),
            pltpu.VMEM((width, depth), BF16),
            pltpu.VMEM((3, tokens, width), F32),
            pltpu.SemaphoreType.DMA((3,)),
            pltpu.SemaphoreType.DMA((13,)),
            pltpu.SemaphoreType.DMA((64,)),
        ],
        cost_estimate=_cost(
            flops=6 * tokens * depth * width, bytes_accessed=6 * depth * width + 8 * depth * tokens, transcendentals=0
        ),
    )(ids, *xs, *gs, wg, wu, wd)


def _chip_body(width, mine, o0, o1, o2, chip, code, tick):
    tick[...] = jnp.zeros_like(tick)
    for i in range(3):
        cols = slice(i * width, (i + 1) * width)
        total = mine[:, cols] + (o0, o1, o2)[i][...]
        chip[:, cols] = total
        size = jnp.abs(total)
        top = jnp.max(jnp.max(size, axis=0, keepdims=True), axis=1, keepdims=True)
        top = jnp.maximum(top * 1.01, 1e-35).astype(BF16).astype(F32)
        code[:, cols] = encode(jnp.sqrt(size * (1.0 / top)), total >= 0)
        code[16 * i : 16 * i + 16, 3 * width :] = jnp.broadcast_to(top, (16, 128)).astype(BF16)
    code[48:, 3 * width :] = jnp.zeros((code.shape[0] - 48, 128), BF16)


def chip_sum(mine, others):
    rows, three = mine.shape
    return _call(
        functools.partial(_chip_body, three // 3),
        (shape((rows, three), F32), shape((rows, three + 128), BF16), TICK),
        in_specs=[VMEM] * 4,
        out_specs=(VMEM,) * 3,
        cost_estimate=_cost(
            flops=20 * rows * three, bytes_accessed=14 * rows * three, transcendentals=2 * rows * three
        ),
    )(mine, *others)


def _act_body(width, chip, code, _, o0, o1, o2):
    def whole(i):
        cols = slice(i * width, (i + 1) * width)
        u, positive = decode(code[:, cols])
        top = code[16 * i : 16 * i + 16, 3 * width :].astype(F32)[0:1, 0:1]
        return chip[:, cols] + _signed(u * u * top, positive)

    gate, up, grad_hidden = whole(0), whole(1), whole(2)
    squash = 1.0 / (1.0 + jnp.exp(-gate))
    o0[...] = gate * squash * up
    o1[...] = grad_hidden * up * squash * (1.0 + gate * (1.0 - squash))
    o2[...] = grad_hidden * gate * squash


def activations(chip, code, after):
    rows, three = chip.shape
    return _call(
        functools.partial(_act_body, three // 3),
        (shape((rows, three // 3), F32),) * 3,
        in_specs=[VMEM] * 2 + [ANY],
        out_specs=(VMEM,) * 3,
        cost_estimate=_cost(
            flops=20 * rows * three, bytes_accessed=10 * rows * three, transcendentals=2 * rows * three
        ),
    )(chip, code, after)


def _pack(block):
    size = jnp.abs(block)
    top = jnp.maximum(jnp.max(size, axis=0, keepdims=True) * 1.01, 1e-35)
    top = top.astype(BF16).astype(F32)
    return encode(size * (1.0 / top), block >= 0), top


def _unpack(code, top):
    u, positive = decode(code)
    return _signed(u * top, positive)


def _grad_in_body(width, n_before, ids, wg, wu, m0, m1, m2, o0, o1, o2, *rest):
    before, (pair_out, own, c1, c2, c3, tick, pair, right, tops, blocks, codes, sem) = rest[:n_before], rest[n_before:]
    core, s1 = ids[0], ids[2]
    half = m0.shape[0]
    tokens = 2 * half
    tick[...] = jnp.zeros_like(tick)
    for parts, place in (((m0, m1, m2), core), ((o0, o1, o2), 1 - core)):
        rows = pl.ds(pl.multiple_of(place * half, half), half)
        rest = pl.ds(pl.multiple_of(tokens + place * half, half), half)
        for i, part in enumerate(parts):
            value = part[...]
            high = value.astype(BF16)
            low = (value - high.astype(F32)).astype(BF16)
            pair[rows, i * width : (i + 1) * width] = high
            pair[rest, i * width : (i + 1) * width] = low
            if i:
                right[rows, (2 * i - 2) * width : (2 * i - 1) * width] = high
                right[rows, (2 * i - 1) * width : 2 * i * width] = low
    store = pltpu.make_async_copy(pair, pair_out, sem)
    store.start()
    for part in range(4):
        some = slice(part * 512, (part + 1) * 512)
        g, u = wg[some, :], wu[some, :]
        total = lax.dot_general(
            jnp.concatenate([g, g, u, u], axis=1), right[...], (((1,), (1,)), ((), ())), preferred_element_type=F32
        )
        for sub in range(8):
            at, x = part * 2 + sub // 4, sub % 4
            y, z = at // 4, at % 4
            block = total[sub * 64 : (sub + 1) * 64]
            k = lax.rem(jnp.where(core == 0, x, z) - s1 + 4, 4)
            j = jnp.where(core == 0, at, y * 4 + x)
            rows = pl.ds(pl.multiple_of(j * 64, 64), 64)
            code, scale = _pack(block)
            tops[pl.ds(k, 1), pl.ds(j, 1), :] = scale[None]
            blocks[pl.ds(k, 1), rows, :] = block[None]
            codes[pl.ds(k, 1), rows, :] = code[None]
    for out, earlier in zip((own, c1, c2, c3), before):
        out[0] = earlier[0]
    c = own.shape[0] - 1
    own[c] = blocks[0]
    for n, out in ((1, c1), (2, c2), (3, c3)):
        out[c, 0:512, :] = codes[n]
        out[c, 512:528, :] = jnp.concatenate([tops[n], tops[n]], axis=0).astype(BF16)
    store.wait()


def grad_in(ids, wg, wu, mine, theirs, before):
    half, width = mine[0].shape
    tokens, three = 2 * half, 3 * width
    n = 1 + (len(before) > 0)
    code = shape((n, 528, tokens), BF16)
    return _call(
        functools.partial(_grad_in_body, width, len(before)),
        (shape((2 * tokens, three), BF16), shape((n, 512, tokens), F32), code, code, code, TICK),
        LARGE,
        in_specs=[SMEM] + [VMEM] * (8 + len(before)),
        out_specs=(ANY,) + (VMEM,) * 5,
        scratch_shapes=[
            pltpu.VMEM((2 * tokens, three), BF16),
            pltpu.VMEM((tokens, 4 * width), BF16),
            pltpu.VMEM((4, 8, tokens), F32),
            pltpu.VMEM((4, 512, tokens), F32),
            pltpu.VMEM((4, 512, tokens), BF16),
            pltpu.SemaphoreType.DMA,
        ],
        cost_estimate=_cost(
            flops=8 * tokens * 2048 * width, bytes_accessed=4 * 2048 * width + 16 * tokens * three, transcendentals=2048 * tokens
        ),
    )(ids, wg, wu, *mine, *theirs, *before)


def _twice(rows, c):
    half = rows.shape[1] // 2
    part = rows[:, c * half : (c + 1) * half]
    return jnp.concatenate([part, part], axis=1)


def _grad_up_body(x, d0, d1, out):
    rows = x[0]
    total = jnp.dot(_twice(rows, 0), d0[...], preferred_element_type=F32)
    total = total + jnp.dot(_twice(rows, 1), d1[...], preferred_element_type=F32)
    out[...] = total.astype(BF16)


def grad_weight(acts, pairs, place, width):
    depth, tokens = acts.shape[1:]
    delta = pl.BlockSpec((tokens, width), lambda i: (0, place))
    return _call(
        _grad_up_body,
        shape((depth, width), BF16),
        WHOLE,
        grid=(depth // 512,),
        in_specs=[pl.BlockSpec((1, 512, tokens), lambda i: (0, i, 0))] + [delta] * 2,
        out_specs=pl.BlockSpec((512, width), lambda i: (i, 0)),
        cost_estimate=_cost(
            flops=COST * 4 * tokens * depth * width, bytes_accessed=COST * 4 * depth * width, transcendentals=0
        ),
    )(acts, *pairs)


def _grad_down_body(g, h0, h1, out, turned):
    @pl.when(pl.program_id(0) == 0)
    def _():
        for i, h in enumerate((h0, h1)):
            turned[i] = h[...].T

    rows, dims = g[0], (((1,), (1,)), ((), ()))
    total = lax.dot_general(turned[0], _twice(rows, 0), dims, preferred_element_type=F32)
    total = total + lax.dot_general(turned[1], _twice(rows, 1), dims, preferred_element_type=F32)
    out[...] = total.astype(BF16)


def grad_down_weight(acts, pairs, width):
    depth, tokens = acts.shape[1:]
    hidden = pl.BlockSpec((tokens, width), lambda i: (0, 0))
    return _call(
        _grad_down_body,
        shape((width, depth), BF16),
        WHOLE,
        grid=(depth // 512,),
        in_specs=[pl.BlockSpec((1, 512, tokens), lambda i: (1, i, 0))] + [hidden] * 2,
        out_specs=pl.BlockSpec((width, 512), lambda i: (0, i)),
        scratch_shapes=[pltpu.VMEM((2, width, tokens), BF16)],
        cost_estimate=_cost(
            flops=COST * 4 * tokens * depth * width, bytes_accessed=COST * 4 * depth * width, transcendentals=0
        ),
    )(acts, *pairs)


def _sum_first_body(ids, own, r1, r2, r3, own2, c1, c2, c3, tops):
    s2 = ids[3]
    for c in range(2):
        scales = [r[c, 512:528, :].astype(F32) for r in (r1, r2, r3)]
        for j in range(8):
            rows = slice(j * 64, (j + 1) * 64)
            total = own[c, rows, :]
            for r, scale in zip((r1, r2, r3), scales):
                total = total + _unpack(r[c, rows, :], scale[j : j + 1])
            y, place = j // 4, j % 4
            k = lax.rem(place - s2 + 4, 4)
            code, scale = _pack(total)
            tops[pl.ds(k, 1), y : y + 1, :] = scale[None]
            to = slice(y * 64, (y + 1) * 64)

            @pl.when(k == 0)
            def _():
                own2[c, to, :] = total

            for n, out in ((1, c1), (2, c2), (3, c3)):

                @pl.when(k == n)
                def _():
                    out[c, to, :] = code

        for n, out in ((1, c1), (2, c2), (3, c3)):
            out[c, 128:144, :] = jnp.concatenate([tops[n], tops[n]], axis=0).astype(BF16)


def sum_first(ids, own, received):
    tokens = own.shape[2]
    code = shape((2, 144, tokens), BF16)
    return _call(
        _sum_first_body,
        (shape((2, 128, tokens), F32), code, code, code),
        in_specs=[SMEM] + [VMEM] * 4,
        out_specs=(VMEM,) * 4,
        scratch_shapes=[pltpu.VMEM((4, 8, tokens), F32)],
    )(ids, own, *received)


def _sum_second_body(ids, own, r1, r2, r3, own3, out):
    for c in range(2):
        scales = [r[c, 128:144, :].astype(F32) for r in (r1, r2, r3)]
        for y in range(2):
            rows = slice(y * 64, (y + 1) * 64)
            total = own[c, rows, :]
            for r, scale in zip((r1, r2, r3), scales):
                total = total + _unpack(r[c, rows, :], scale[y : y + 1])

            @pl.when(ids[1] == y)
            def _():
                own3[c] = total

            @pl.when(ids[1] != y)
            def _():
                code, top = _pack(total)
                out[c, 0:64, :] = code
                out[c, 64:80, :] = jnp.broadcast_to(top, (16, top.shape[1])).astype(BF16)


def sum_second(ids, own, received):
    tokens = own.shape[2]
    return _call(
        _sum_second_body,
        (shape((2, 64, tokens), F32), shape((2, 80, tokens), BF16)),
        in_specs=[SMEM] + [VMEM] * 4,
        out_specs=(VMEM,) * 2,
    )(ids, own, *received)


def _sum_last_body(own, r, out):
    tokens = own.shape[2]
    for c in range(2):
        total = own[c] + _unpack(r[c, 0:64, :], r[c, 64:80, :].astype(F32)[0:1])
        out[:, c * tokens : (c + 1) * tokens] = total.astype(BF16)


def sum_last(own, received):
    return _call(
        _sum_last_body, shape((64, 2 * own.shape[2]), BF16), in_specs=[VMEM] * 2, out_specs=VMEM
    )(own, received)


def per_device(inputs, grad_out, gate_weight, up_weight, down_weight):
    width = gate_weight.shape[1]
    mp = lax.axis_index("mp")
    core = lax.axis_index("dp") % 2
    y, z, x = mp // 16, (mp // 4) % 4, mp % 4
    ids = jnp.stack([core, y, jnp.where(core == 0, x, z), jnp.where(core == 0, z, x)]).astype(jnp.int32)
    both = jnp.stack([inputs.T, grad_out.T])
    pair = jnp.stack([both, _send(both, _over_y)])
    near = [pair] + [_send(pair, _first(-k)) for k in (1, 2, 3)]
    x, g = (jnp.stack([p[:, i] for p in near]) for i in range(2))
    x1, g3 = _send(x, _second(-1)), _send(g, _second(1))
    g1, x3 = _send(g, _second(-1)), _send(x, _second(1))
    x2, g2 = _send(x1, _second(-1)), _send(g3, _second(1))
    mine0, mine1, *theirs, acts = forward(
        ids, (x, x1, x2, x3), (g, g1, g2, g3), gate_weight, up_weight, down_weight
    )
    chips, codes = [], []
    for mine, others in ((mine0, theirs[:3]), (mine1, theirs[3:])):
        chip, code, tick = chip_sum(mine, [_send(v, _over_core) for v in others])
        chips.append(chip)
        codes.append(_send(code, _over_lo))
    pairs, part = [], ()
    for chip, code in zip(chips, codes):
        act = activations(chip, code, tick)
        others = [_send(v, _over_core) for v in act]
        delta, *part, tick = grad_in(ids, gate_weight, up_weight, act, others, part)
        pairs.append(delta)
    own, *rest = part
    own, *rest = sum_first(ids, own, [_send(v, _first(k + 1)) for k, v in enumerate(rest)])
    own, last = sum_second(ids, own, [_send(v, _second(k + 1)) for k, v in enumerate(rest)])
    grad_inputs = sum_last(own, _send(last, _over_y)).T
    grad_gate = grad_weight(acts, pairs, 1, width)
    grad_up = grad_weight(acts, pairs, 2, width)
    grad_down = grad_down_weight(acts, pairs, width)
    return (grad_inputs, grad_gate, grad_up, grad_down)


def solution(mesh):
    placed = (
        P(None, ("dp", "mp")),
        P(None, ("dp", "mp")),
        P("dp", "mp"),
        P("dp", "mp"),
        P("mp", "dp"),
    )
    return jax.shard_map(
        per_device,
        mesh=mesh,
        in_specs=placed,
        out_specs=(P(None, ("dp", "mp")), P("dp", "mp"), P("dp", "mp"), P("mp", "dp")),
        check_vma=False,
    )
```

```python
import functools

import jax
import jax.numpy as jnp
from jax import lax
from jax.experimental import pallas as pl
from jax.experimental.pallas import tpu as pltpu
from jax.sharding import PartitionSpec as P

COST = 20
F32, BF16 = jnp.float32, jnp.bfloat16
SMALL, LARGE, WHOLE = 16 * 1024 * 1024, 40 * 1024 * 1024, 60 * 1024 * 1024
BOTH = ("dp", "mp")


def _moves(shift):
    pairs = []
    for i in range(128):
        lo, core, y, z, x = i // 64, (i // 32) % 2, (i // 16) % 2, (i // 4) % 4, i % 4
        lo, core, y, z, x = shift(lo, core, y, z, x)
        pairs.append((i, (lo % 2) * 64 + (core % 2) * 32 + (y % 2) * 16 + (z % 4) * 4 + x % 4))
    return pairs


def _send(a, shift):
    return lax.ppermute(a, BOTH, _moves(shift))


def _first(k):
    return lambda lo, c, y, z, x: (lo, c, y, z + k * c, x + k * (1 - c))


def _second(k):
    return lambda lo, c, y, z, x: (lo, c, y, z + k * (1 - c), x + k * c)


def _over_y(lo, c, y, z, x):
    return lo, c, y + 1, z, x


def _over_core(lo, c, y, z, x):
    return lo, c + 1, y, z, x


def _over_lo(lo, c, y, z, x):
    return lo + 1, c, y, z, x


def encode(u, positive):
    code = jnp.exp2(u * 200.0 - 100.0)
    return jnp.where(positive, code, -code).astype(BF16)


def decode(code):
    wide = code.astype(F32)
    return (jnp.log2(jnp.abs(wide)) + 100.0) * (1.0 / 200.0), wide > 0


def _signed(value, positive):
    return jnp.where(positive, value, -value)


def _call(body, out, room=SMALL, **kw):
    params = pltpu.CompilerParams(vmem_limit_bytes=room)
    return pl.pallas_call(body, out_shape=out, compiler_params=params, **kw)


def _cost(flops, bytes_accessed, transcendentals):
    return pl.CostEstimate(
        flops=flops // COST, bytes_accessed=bytes_accessed // COST, transcendentals=transcendentals // COST
    )


SMEM = pl.BlockSpec(memory_space=pltpu.SMEM)
VMEM = pl.BlockSpec(memory_space=pltpu.VMEM)
ANY = pl.BlockSpec(memory_space=pl.ANY)


def shape(dims, dtype):
    return jax.ShapeDtypeStruct(dims, dtype)


TICK = shape((8, 128), F32)


def _forward_body(n, width, ids, *rest):
    pieces, weights, rest = rest[:4], rest[4 : 4 + n], rest[4 + n :]
    mine, theirs, rest = rest[:2], rest[2 : 2 + 2 * n], rest[2 + 2 * n :]
    acts_out, acts, turned, held, sums, loads, stores, sems = rest
    loading = [pltpu.make_async_copy(weight, held.at[i], loads.at[i]) for i, weight in enumerate(weights)]
    core, y, s1, s2 = ids[0], ids[1], ids[2], ids[3]
    copies = []
    for k2, piece in enumerate(pieces):
        b = lax.rem(s2 + k2, 4)
        for k1 in range(4):
            a = lax.rem(s1 + k1, 4)
            zx = jnp.where(core == 0, b * 4 + a, a * 4 + b)
            for k0 in range(2):
                at = pl.multiple_of((lax.rem(y + k0, 2) * 16 + zx) * 64, 64)
                copies.append(
                    pltpu.make_async_copy(piece.at[k1, k0], acts.at[pl.ds(at, 64), :], sems.at[len(copies)])
                )
    for copy in copies:
        copy.start()
    for copy in loading:
        copy.start()
    for copy in copies:
        copy.wait()
    out = [pltpu.make_async_copy(acts, acts_out, stores.at[0])]
    out[0].start()
    half = mine[0].shape[0]
    for m, place in enumerate((core, 1 - core)):
        for c in range(2):
            cols = pl.ds(pl.multiple_of((2 * c + place) * half, half), half)
            row = (2 * m + c) * half
            turned[row : row + half, :] = acts[:, cols].T
    for i in range(n):
        loading[i].wait()
        dims = (((1,), (0,)), ((), ())) if n == 2 else (((1,), (1,)), ((), ()))
        sums[i] = lax.dot_general(turned[...], held[i], dims, preferred_element_type=F32)
        for c in range(2):
            for row, to in (
                (c * half, mine[c].at[:, pl.ds(i * width, width)]),
                ((2 + c) * half, theirs[n * c + i]),
            ):
                copy = pltpu.make_async_copy(sums.at[i, pl.ds(row, half), :], to, stores.at[len(out)])
                copy.start()
                out.append(copy)
    for copy in out:
        copy.wait()


def _whole(*dims):
    return pl.BlockSpec(dims, lambda i: (0,) * len(dims))


def forward(ids, pieces, weights, width):
    n, tokens = len(weights), pieces[0].shape[-1]
    depth = 32 * 64
    mine, other = shape((tokens // 4, n * width), F32), shape((tokens // 4, width), F32)
    *out, acts = _call(
        functools.partial(_forward_body, n, width),
        (mine,) * 2 + (other,) * (2 * n) + (shape((depth, tokens), BF16),),
        WHOLE,
        in_specs=[SMEM] + [ANY] * (4 + n),
        out_specs=(ANY,) * (3 + 2 * n),
        scratch_shapes=[
            pltpu.VMEM((depth, tokens), BF16),
            pltpu.VMEM((tokens, depth), BF16),
            pltpu.VMEM((n, *weights[0].shape), BF16),
            pltpu.VMEM((n, tokens, width), F32),
            pltpu.SemaphoreType.DMA((n,)),
            pltpu.SemaphoreType.DMA((1 + 4 * n,)),
            pltpu.SemaphoreType.DMA((32,)),
        ],
        cost_estimate=_cost(
            flops=2 * n * tokens * depth * width, bytes_accessed=2 * n * depth * width + 4 * depth * tokens, transcendentals=0
        ),
    )(ids, *pieces, *weights)
    return (out[0], out[2 : 2 + n]), (out[1], out[2 + n :]), acts


def _chip_body(n, width, mine, *rest):
    others, (chip, code, tick) = rest[:n], rest[n:]
    tick[...] = jnp.zeros_like(tick)
    for i in range(n):
        cols = slice(i * width, (i + 1) * width)
        total = mine[:, cols] + others[i][...]
        chip[:, cols] = total
        size = jnp.abs(total)
        top = jnp.max(jnp.max(size, axis=0, keepdims=True), axis=1, keepdims=True)
        top = jnp.maximum(top * 1.01, 1e-35).astype(BF16).astype(F32)
        code[:, cols] = encode(jnp.sqrt(size * (1.0 / top)), total >= 0)
        code[16 * i : 16 * i + 16, n * width :] = jnp.broadcast_to(top, (16, 128)).astype(BF16)
    code[16 * n :, n * width :] = jnp.zeros((code.shape[0] - 16 * n, 128), BF16)


def chip_sum(mine, others):
    (rows, whole), n = mine.shape, len(others)
    return _call(
        functools.partial(_chip_body, n, whole // n),
        (shape((rows, whole), F32), shape((rows, whole + 128), BF16), TICK),
        in_specs=[VMEM] * (1 + n),
        out_specs=(VMEM,) * 3,
        cost_estimate=_cost(
            flops=20 * rows * whole, bytes_accessed=14 * rows * whole, transcendentals=2 * rows * whole
        ),
    )(mine, *others)


def _act_body(width, chip, code, chip_h, code_h, _, o0, o1, o2):
    def total(part, coded, i, n):
        cols = slice(i * width, (i + 1) * width)
        u, positive = decode(coded[:, cols])
        top = coded[16 * i : 16 * i + 16, n * width :].astype(F32)[0:1, 0:1]
        return part[:, cols] + _signed(u * u * top, positive)

    gate, up, grad_hidden = total(chip, code, 0, 2), total(chip, code, 1, 2), total(chip_h, code_h, 0, 1)
    squash = 1.0 / (1.0 + jnp.exp(-gate))
    o0[...] = gate * squash * up
    o1[...] = grad_hidden * up * squash * (1.0 + gate * (1.0 - squash))
    o2[...] = grad_hidden * gate * squash


def activations(chip, code, chip_h, code_h, after):
    rows, width = chip_h.shape
    return _call(
        functools.partial(_act_body, width),
        (shape((rows, width), F32),) * 3,
        in_specs=[VMEM] * 4 + [ANY],
        out_specs=(VMEM,) * 3,
        cost_estimate=_cost(
            flops=60 * rows * width, bytes_accessed=30 * rows * width, transcendentals=6 * rows * width
        ),
    )(chip, code, chip_h, code_h, after)


def _pack(block):
    size = jnp.abs(block)
    top = jnp.maximum(jnp.max(size, axis=0, keepdims=True) * 1.01, 1e-35)
    top = top.astype(BF16).astype(F32)
    return encode(size * (1.0 / top), block >= 0), top


def _unpack(code, top):
    u, positive = decode(code)
    return _signed(u * top, positive)


def _grad_in_body(width, n_before, ids, wg, wu, m0, m1, m2, o0, o1, o2, *rest):
    before, (pair_out, own, c1, c2, c3, tick, pair, right, tops, blocks, codes, sem) = rest[:n_before], rest[n_before:]
    core, s1 = ids[0], ids[2]
    half = m0.shape[0]
    tokens = 2 * half
    tick[...] = jnp.zeros_like(tick)
    for parts, place in (((m0, m1, m2), core), ((o0, o1, o2), 1 - core)):
        rows = pl.ds(pl.multiple_of(place * half, half), half)
        rest = pl.ds(pl.multiple_of(tokens + place * half, half), half)
        for i, part in enumerate(parts):
            value = part[...]
            high = value.astype(BF16)
            low = (value - high.astype(F32)).astype(BF16)
            pair[rows, i * width : (i + 1) * width] = high
            pair[rest, i * width : (i + 1) * width] = low
            if i:
                right[rows, (2 * i - 2) * width : (2 * i - 1) * width] = high
                right[rows, (2 * i - 1) * width : 2 * i * width] = low
    store = pltpu.make_async_copy(pair, pair_out, sem)
    store.start()
    for part in range(4):
        some = slice(part * 512, (part + 1) * 512)
        g, u = wg[some, :], wu[some, :]
        total = lax.dot_general(
            jnp.concatenate([g, g, u, u], axis=1), right[...], (((1,), (1,)), ((), ())), preferred_element_type=F32
        )
        for sub in range(8):
            at, x = part * 2 + sub // 4, sub % 4
            y, z = at // 4, at % 4
            block = total[sub * 64 : (sub + 1) * 64]
            k = lax.rem(jnp.where(core == 0, x, z) - s1 + 4, 4)
            j = jnp.where(core == 0, at, y * 4 + x)
            rows = pl.ds(pl.multiple_of(j * 64, 64), 64)
            code, scale = _pack(block)
            tops[pl.ds(k, 1), pl.ds(j, 1), :] = scale[None]
            blocks[pl.ds(k, 1), rows, :] = block[None]
            codes[pl.ds(k, 1), rows, :] = code[None]
    for out, earlier in zip((own, c1, c2, c3), before):
        out[0] = earlier[0]
    c = own.shape[0] - 1
    own[c] = blocks[0]
    for n, out in ((1, c1), (2, c2), (3, c3)):
        out[c, 0:512, :] = codes[n]
        out[c, 512:528, :] = jnp.concatenate([tops[n], tops[n]], axis=0).astype(BF16)
    store.wait()


def grad_in(ids, wg, wu, mine, theirs, before):
    half, width = mine[0].shape
    tokens, three = 2 * half, 3 * width
    n = 1 + (len(before) > 0)
    code = shape((n, 528, tokens), BF16)
    return _call(
        functools.partial(_grad_in_body, width, len(before)),
        (shape((2 * tokens, three), BF16), shape((n, 512, tokens), F32), code, code, code, TICK),
        LARGE,
        in_specs=[SMEM] + [VMEM] * (8 + len(before)),
        out_specs=(ANY,) + (VMEM,) * 5,
        scratch_shapes=[
            pltpu.VMEM((2 * tokens, three), BF16),
            pltpu.VMEM((tokens, 4 * width), BF16),
            pltpu.VMEM((4, 8, tokens), F32),
            pltpu.VMEM((4, 512, tokens), F32),
            pltpu.VMEM((4, 512, tokens), BF16),
            pltpu.SemaphoreType.DMA,
        ],
        cost_estimate=_cost(
            flops=8 * tokens * 2048 * width, bytes_accessed=4 * 2048 * width + 16 * tokens * three, transcendentals=2048 * tokens
        ),
    )(ids, wg, wu, *mine, *theirs, *before)


def _twice(rows, c):
    half = rows.shape[1] // 2
    part = rows[:, c * half : (c + 1) * half]
    return jnp.concatenate([part, part], axis=1)


def _grad_up_body(x, d0, d1, out):
    rows = x[...]
    total = jnp.dot(_twice(rows, 0), d0[...], preferred_element_type=F32)
    total = total + jnp.dot(_twice(rows, 1), d1[...], preferred_element_type=F32)
    out[...] = total.astype(BF16)


def grad_weight(part, pairs, place, width):
    depth, tokens = part.shape
    delta = pl.BlockSpec((tokens, width), lambda i: (0, place))
    return _call(
        _grad_up_body,
        shape((depth, width), BF16),
        WHOLE,
        grid=(depth // 512,),
        in_specs=[pl.BlockSpec((512, tokens), lambda i: (i, 0))] + [delta] * 2,
        out_specs=pl.BlockSpec((512, width), lambda i: (i, 0)),
        cost_estimate=_cost(
            flops=COST * 4 * tokens * depth * width, bytes_accessed=COST * 4 * depth * width, transcendentals=0
        ),
    )(part, *pairs)


def _grad_down_body(g, h0, h1, out, turned):
    @pl.when(pl.program_id(0) == 0)
    def _():
        for i, h in enumerate((h0, h1)):
            turned[i] = h[...].T

    rows, dims = g[...], (((1,), (1,)), ((), ()))
    total = lax.dot_general(turned[0], _twice(rows, 0), dims, preferred_element_type=F32)
    total = total + lax.dot_general(turned[1], _twice(rows, 1), dims, preferred_element_type=F32)
    out[...] = total.astype(BF16)


def grad_down_weight(part, pairs, width):
    depth, tokens = part.shape
    hidden = pl.BlockSpec((tokens, width), lambda i: (0, 0))
    return _call(
        _grad_down_body,
        shape((width, depth), BF16),
        WHOLE,
        grid=(depth // 512,),
        in_specs=[pl.BlockSpec((512, tokens), lambda i: (i, 0))] + [hidden] * 2,
        out_specs=pl.BlockSpec((width, 512), lambda i: (0, i)),
        scratch_shapes=[pltpu.VMEM((2, width, tokens), BF16)],
        cost_estimate=_cost(
            flops=COST * 4 * tokens * depth * width, bytes_accessed=COST * 4 * depth * width, transcendentals=0
        ),
    )(part, *pairs)


def _sum_first_body(ids, own, r1, r2, r3, own2, c1, c2, c3, tops):
    s2 = ids[3]
    for c in range(2):
        scales = [r[c, 512:528, :].astype(F32) for r in (r1, r2, r3)]
        for j in range(8):
            rows = slice(j * 64, (j + 1) * 64)
            total = own[c, rows, :]
            for r, scale in zip((r1, r2, r3), scales):
                total = total + _unpack(r[c, rows, :], scale[j : j + 1])
            y, place = j // 4, j % 4
            k = lax.rem(place - s2 + 4, 4)
            code, scale = _pack(total)
            tops[pl.ds(k, 1), y : y + 1, :] = scale[None]
            to = slice(y * 64, (y + 1) * 64)

            @pl.when(k == 0)
            def _():
                own2[c, to, :] = total

            for n, out in ((1, c1), (2, c2), (3, c3)):

                @pl.when(k == n)
                def _():
                    out[c, to, :] = code

        for n, out in ((1, c1), (2, c2), (3, c3)):
            out[c, 128:144, :] = jnp.concatenate([tops[n], tops[n]], axis=0).astype(BF16)


def sum_first(ids, own, received):
    tokens = own.shape[2]
    code = shape((2, 144, tokens), BF16)
    return _call(
        _sum_first_body,
        (shape((2, 128, tokens), F32), code, code, code),
        in_specs=[SMEM] + [VMEM] * 4,
        out_specs=(VMEM,) * 4,
        scratch_shapes=[pltpu.VMEM((4, 8, tokens), F32)],
    )(ids, own, *received)


def _sum_second_body(ids, own, r1, r2, r3, own3, out):
    for c in range(2):
        scales = [r[c, 128:144, :].astype(F32) for r in (r1, r2, r3)]
        for y in range(2):
            rows = slice(y * 64, (y + 1) * 64)
            total = own[c, rows, :]
            for r, scale in zip((r1, r2, r3), scales):
                total = total + _unpack(r[c, rows, :], scale[y : y + 1])

            @pl.when(ids[1] == y)
            def _():
                own3[c] = total

            @pl.when(ids[1] != y)
            def _():
                code, top = _pack(total)
                out[c, 0:64, :] = code
                out[c, 64:80, :] = jnp.broadcast_to(top, (16, top.shape[1])).astype(BF16)


def sum_second(ids, own, received):
    tokens = own.shape[2]
    return _call(
        _sum_second_body,
        (shape((2, 64, tokens), F32), shape((2, 80, tokens), BF16)),
        in_specs=[SMEM] + [VMEM] * 4,
        out_specs=(VMEM,) * 2,
    )(ids, own, *received)


def _sum_last_body(own, r, out):
    tokens = own.shape[2]
    for c in range(2):
        total = own[c] + _unpack(r[c, 0:64, :], r[c, 64:80, :].astype(F32)[0:1])
        out[:, c * tokens : (c + 1) * tokens] = total.astype(BF16)


def sum_last(own, received):
    return _call(
        _sum_last_body, shape((64, 2 * own.shape[2]), BF16), in_specs=[VMEM] * 2, out_specs=VMEM
    )(own, received)


def per_device(inputs, grad_out, gate_weight, up_weight, down_weight):
    width = gate_weight.shape[1]
    mp = lax.axis_index("mp")
    core = lax.axis_index("dp") % 2
    y, z, x = mp // 16, (mp // 4) % 4, mp % 4
    ids = jnp.stack([core, y, jnp.where(core == 0, x, z), jnp.where(core == 0, z, x)]).astype(jnp.int32)
    both = jnp.stack([inputs.T, grad_out.T])
    pair = jnp.stack([both, _send(both, _over_y)])
    near = [pair] + [_send(pair, _first(-k)) for k in (1, 2, 3)]
    x, g = (jnp.stack([p[:, i] for p in near]) for i in range(2))
    x1, x3 = _send(x, _second(-1)), _send(x, _second(1))
    x2 = _send(x1, _second(-1))
    g3, g1 = _send(g, _second(1)), _send(g, _second(-1))
    g2 = _send(g3, _second(1))

    def exchange(mine, others):
        chip, code, tick = chip_sum(mine, [_send(v, _over_core) for v in others])
        return (chip, _send(code, _over_lo)), tick

    *ups, x_acts = forward(ids, (x, x1, x2, x3), (gate_weight, up_weight), width)
    ups = [exchange(*part)[0] for part in ups]
    *downs, g_acts = forward(ids, (g, g1, g2, g3), (down_weight,), width)
    downs = [exchange(*part) for part in downs]
    tick = downs[1][1]
    pairs, part = [], ()
    for c in range(2):
        act = activations(*ups[c], *downs[c][0], tick)
        others = [_send(v, _over_core) for v in act]
        delta, *part, tick = grad_in(ids, gate_weight, up_weight, act, others, part)
        pairs.append(delta)
    own, *rest = part
    own, *rest = sum_first(ids, own, [_send(v, _first(k + 1)) for k, v in enumerate(rest)])
    own, last = sum_second(ids, own, [_send(v, _second(k + 1)) for k, v in enumerate(rest)])
    grad_inputs = sum_last(own, _send(last, _over_y)).T
    grad_gate = grad_weight(x_acts, pairs, 1, width)
    grad_up = grad_weight(x_acts, pairs, 2, width)
    grad_down = grad_down_weight(g_acts, pairs, width)
    return (grad_inputs, grad_gate, grad_up, grad_down)


def solution(mesh):
    placed = (
        P(None, ("dp", "mp")),
        P(None, ("dp", "mp")),
        P("dp", "mp"),
        P("dp", "mp"),
        P("mp", "dp"),
    )
    return jax.shard_map(
        per_device,
        mesh=mesh,
        in_specs=placed,
        out_specs=(P(None, ("dp", "mp")), P("dp", "mp"), P("dp", "mp"), P("mp", "dp")),
        check_vma=False,
    )
```

```python
import functools

import jax
import jax.numpy as jnp
from jax import lax
from jax.experimental import pallas as pl
from jax.experimental.pallas import tpu as pltpu
from jax.sharding import PartitionSpec as P

COST = 20
F32, BF16 = jnp.float32, jnp.bfloat16
SMALL, DELTA, WHOLE = 16 * 1024 * 1024, 40 * 1024 * 1024, 60 * 1024 * 1024
BOTH = ("dp", "mp")


def _moves(shift):
    pairs = []
    for i in range(128):
        lo, core, y, z, x = i // 64, (i // 32) % 2, (i // 16) % 2, (i // 4) % 4, i % 4
        lo, core, y, z, x = shift(lo, core, y, z, x)
        pairs.append((i, (lo % 2) * 64 + (core % 2) * 32 + (y % 2) * 16 + (z % 4) * 4 + x % 4))
    return pairs


def _send(a, shift):
    return lax.ppermute(a, BOTH, _moves(shift))


def _first(k):
    return lambda lo, c, y, z, x: (lo, c, y, z + k * c, x + k * (1 - c))


def _second(k):
    return lambda lo, c, y, z, x: (lo, c, y, z + k * (1 - c), x + k * c)


def _over_y(lo, c, y, z, x):
    return lo, c, y + 1, z, x


def _over_core(lo, c, y, z, x):
    return lo, c + 1, y, z, x


def _over_lo(lo, c, y, z, x):
    return lo + 1, c, y, z, x


def encode(u, positive):
    code = jnp.exp2(u * 200.0 - 100.0)
    return jnp.where(positive, code, -code).astype(BF16)


def decode(code):
    wide = code.astype(F32)
    return (jnp.log2(jnp.abs(wide)) + 100.0) * (1.0 / 200.0), wide > 0


def _signed(value, positive):
    return jnp.where(positive, value, -value)


def _call(body, out, room=SMALL, **kw):
    params = pltpu.CompilerParams(vmem_limit_bytes=room)
    return pl.pallas_call(body, out_shape=out, compiler_params=params, **kw)


def _cost(flops, bytes_accessed, transcendentals):
    return pl.CostEstimate(
        flops=flops // COST, bytes_accessed=bytes_accessed // COST, transcendentals=transcendentals // COST
    )


SMEM = pl.BlockSpec(memory_space=pltpu.SMEM)
VMEM = pl.BlockSpec(memory_space=pltpu.VMEM)
ANY = pl.BlockSpec(memory_space=pl.ANY)


def shape(dims, dtype):
    return jax.ShapeDtypeStruct(dims, dtype)


TICK = shape((8, 128), F32)


def _forward_body(n, width, ids, *rest):
    pieces, weights, rest = rest[:4], rest[4 : 4 + n], rest[4 + n :]
    mine, theirs, rest = rest[:2], rest[2 : 2 + 2 * n], rest[2 + 2 * n :]
    acts_out, acts, turned, held, sums, loads, stores, sems = rest
    loading = [pltpu.make_async_copy(weight, held.at[i], loads.at[i]) for i, weight in enumerate(weights)]
    core, y, s1, s2 = ids[0], ids[1], ids[2], ids[3]
    copies = []
    for k2, piece in enumerate(pieces):
        b = lax.rem(s2 + k2, 4)
        for k1 in range(4):
            a = lax.rem(s1 + k1, 4)
            zx = jnp.where(core == 0, b * 4 + a, a * 4 + b)
            for k0 in range(2):
                at = pl.multiple_of((lax.rem(y + k0, 2) * 16 + zx) * 64, 64)
                copies.append(
                    pltpu.make_async_copy(piece.at[k1, k0], acts.at[pl.ds(at, 64), :], sems.at[len(copies)])
                )
    for copy in copies:
        copy.start()
    for copy in loading:
        copy.start()
    for copy in copies:
        copy.wait()
    out = [pltpu.make_async_copy(acts, acts_out, stores.at[0])]
    out[0].start()
    half = mine[0].shape[0]
    for m, place in enumerate((core, 1 - core)):
        for c in range(2):
            cols = pl.ds(pl.multiple_of((2 * c + place) * half, half), half)
            row = (2 * m + c) * half
            turned[row : row + half, :] = acts[:, cols].T
    for i in range(n):
        loading[i].wait()
        dims = (((1,), (0,)), ((), ())) if n == 2 else (((1,), (1,)), ((), ()))
        sums[i] = lax.dot_general(turned[...], held[i], dims, preferred_element_type=F32)
        for c in range(2):
            for row, to in (
                (c * half, mine[c].at[:, pl.ds(i * width, width)]),
                ((2 + c) * half, theirs[n * c + i]),
            ):
                copy = pltpu.make_async_copy(sums.at[i, pl.ds(row, half), :], to, stores.at[len(out)])
                copy.start()
                out.append(copy)
    for copy in out:
        copy.wait()


def _whole(*dims):
    return pl.BlockSpec(dims, lambda i: (0,) * len(dims))


def forward(ids, pieces, weights, width):
    n, tokens = len(weights), pieces[0].shape[-1]
    depth = 32 * 64
    mine, other = shape((tokens // 4, n * width), F32), shape((tokens // 4, width), F32)
    *out, acts = _call(
        functools.partial(_forward_body, n, width),
        (mine,) * 2 + (other,) * (2 * n) + (shape((depth, tokens), BF16),),
        WHOLE,
        in_specs=[SMEM] + [ANY] * (4 + n),
        out_specs=(ANY,) * (3 + 2 * n),
        scratch_shapes=[
            pltpu.VMEM((depth, tokens), BF16),
            pltpu.VMEM((tokens, depth), BF16),
            pltpu.VMEM((n, *weights[0].shape), BF16),
            pltpu.VMEM((n, tokens, width), F32),
            pltpu.SemaphoreType.DMA((n,)),
            pltpu.SemaphoreType.DMA((1 + 4 * n,)),
            pltpu.SemaphoreType.DMA((32,)),
        ],
        cost_estimate=_cost(
            flops=2 * n * tokens * depth * width, bytes_accessed=2 * n * depth * width + 4 * depth * tokens, transcendentals=0
        ),
    )(ids, *pieces, *weights)
    return (out[0], out[2 : 2 + n]), (out[1], out[2 + n :]), acts


def _chip_body(n, width, mine, *rest):
    others, (chip, code, tick) = rest[:n], rest[n:]
    tick[...] = jnp.zeros_like(tick)
    for i in range(n):
        cols = slice(i * width, (i + 1) * width)
        total = mine[:, cols] + others[i][...]
        chip[:, cols] = total
        size = jnp.abs(total)
        top = jnp.max(jnp.max(size, axis=0, keepdims=True), axis=1, keepdims=True)
        top = jnp.maximum(top * 1.01, 1e-35).astype(BF16).astype(F32)
        code[:, cols] = encode(jnp.sqrt(size * (1.0 / top)), total >= 0)
        code[16 * i : 16 * i + 16, n * width :] = jnp.broadcast_to(top, (16, 128)).astype(BF16)
    code[16 * n :, n * width :] = jnp.zeros((code.shape[0] - 16 * n, 128), BF16)


def chip_sum(mine, others):
    (rows, whole), n = mine.shape, len(others)
    return _call(
        functools.partial(_chip_body, n, whole // n),
        (shape((rows, whole), F32), shape((rows, whole + 128), BF16), TICK),
        in_specs=[VMEM] * (1 + n),
        out_specs=(VMEM,) * 3,
        cost_estimate=_cost(
            flops=20 * rows * whole, bytes_accessed=14 * rows * whole, transcendentals=2 * rows * whole
        ),
    )(mine, *others)


def _act_body(width, chip, code, chip_h, code_h, _, o0, o1, o2):
    def total(part, coded, i, n):
        cols = slice(i * width, (i + 1) * width)
        u, positive = decode(coded[:, cols])
        top = coded[16 * i : 16 * i + 16, n * width :].astype(F32)[0:1, 0:1]
        return part[:, cols] + _signed(u * u * top, positive)

    gate, up, grad_hidden = total(chip, code, 0, 2), total(chip, code, 1, 2), total(chip_h, code_h, 0, 1)
    squash = 1.0 / (1.0 + jnp.exp(-gate))
    o0[...] = gate * squash * up
    o1[...] = grad_hidden * up * squash * (1.0 + gate * (1.0 - squash))
    o2[...] = grad_hidden * gate * squash


def activations(chip, code, chip_h, code_h, after):
    rows, width = chip_h.shape
    return _call(
        functools.partial(_act_body, width),
        (shape((rows, width), F32),) * 3,
        in_specs=[VMEM] * 4 + [ANY],
        out_specs=(VMEM,) * 3,
        cost_estimate=_cost(
            flops=60 * rows * width, bytes_accessed=30 * rows * width, transcendentals=6 * rows * width
        ),
    )(chip, code, chip_h, code_h, after)


def _pack(block):
    size = jnp.abs(block)
    top = jnp.maximum(jnp.max(size, axis=0, keepdims=True) * 1.01, 1e-35)
    top = top.astype(BF16).astype(F32)
    return encode(size * (1.0 / top), block >= 0), top


def _unpack(code, top):
    u, positive = decode(code)
    return _signed(u * top, positive)


def _grad_in_body(width, n_before, ids, wg, wu, m0, m1, m2, o0, o1, o2, *rest):
    before, (pair_out, own, c1, c2, c3, tick, pair, right, tops, blocks, codes, sem) = rest[:n_before], rest[n_before:]
    core, s1 = ids[0], ids[2]
    half = m0.shape[0]
    tokens = 2 * half
    tick[...] = jnp.zeros_like(tick)
    for parts, place in (((m0, m1, m2), core), ((o0, o1, o2), 1 - core)):
        rows = pl.ds(pl.multiple_of(place * half, half), half)
        rest = pl.ds(pl.multiple_of(tokens + place * half, half), half)
        for i, part in enumerate(parts):
            value = part[...]
            high = value.astype(BF16)
            low = (value - high.astype(F32)).astype(BF16)
            pair[rows, i * width : (i + 1) * width] = high
            pair[rest, i * width : (i + 1) * width] = low
            if i:
                right[rows, (2 * i - 2) * width : (2 * i - 1) * width] = high
                right[rows, (2 * i - 1) * width : 2 * i * width] = low
    store = pltpu.make_async_copy(pair, pair_out, sem)
    store.start()
    for part in range(4):
        some = slice(part * 512, (part + 1) * 512)
        g, u = wg[some, :], wu[some, :]
        total = lax.dot_general(
            jnp.concatenate([g, g, u, u], axis=1), right[...], (((1,), (1,)), ((), ())), preferred_element_type=F32
        )
        for sub in range(8):
            at, x = part * 2 + sub // 4, sub % 4
            y, z = at // 4, at % 4
            block = total[sub * 64 : (sub + 1) * 64]
            k = lax.rem(jnp.where(core == 0, x, z) - s1 + 4, 4)
            j = jnp.where(core == 0, at, y * 4 + x)
            rows = pl.ds(pl.multiple_of(j * 64, 64), 64)
            code, scale = _pack(block)
            tops[pl.ds(k, 1), pl.ds(j, 1), :] = scale[None]
            blocks[pl.ds(k, 1), rows, :] = block[None]
            codes[pl.ds(k, 1), rows, :] = code[None]
    for out, earlier in zip((own, c1, c2, c3), before):
        out[0] = earlier[0]
    c = own.shape[0] - 1
    own[c] = blocks[0]
    for n, out in ((1, c1), (2, c2), (3, c3)):
        out[c, 0:512, :] = codes[n]
        out[c, 512:528, :] = jnp.concatenate([tops[n], tops[n]], axis=0).astype(BF16)
    store.wait()


def grad_in(ids, wg, wu, mine, theirs, before):
    half, width = mine[0].shape
    tokens, three = 2 * half, 3 * width
    n = 1 + (len(before) > 0)
    code = shape((n, 528, tokens), BF16)
    return _call(
        functools.partial(_grad_in_body, width, len(before)),
        (shape((2 * tokens, three), BF16), shape((n, 512, tokens), F32), code, code, code, TICK),
        DELTA,
        in_specs=[SMEM] + [VMEM] * (8 + len(before)),
        out_specs=(ANY,) + (VMEM,) * 5,
        scratch_shapes=[
            pltpu.VMEM((2 * tokens, three), BF16),
            pltpu.VMEM((tokens, 4 * width), BF16),
            pltpu.VMEM((4, 8, tokens), F32),
            pltpu.VMEM((4, 512, tokens), F32),
            pltpu.VMEM((4, 512, tokens), BF16),
            pltpu.SemaphoreType.DMA,
        ],
        cost_estimate=_cost(
            flops=8 * tokens * 2048 * width, bytes_accessed=4 * 2048 * width + 16 * tokens * three, transcendentals=2048 * tokens
        ),
    )(ids, wg, wu, *mine, *theirs, *before)


def _twice(rows, c):
    half = rows.shape[1] // 2
    part = rows[:, c * half : (c + 1) * half]
    return jnp.concatenate([part, part], axis=1)


def _grad_up_body(steps, x, d0, d1, gate, up, tick):
    tick[...] = jnp.zeros_like(tick)
    rows = x[...]
    total = jnp.dot(_twice(rows, 0), d0[...], preferred_element_type=F32)
    total = total + jnp.dot(_twice(rows, 1), d1[...], preferred_element_type=F32)
    first = pl.program_id(0) < steps

    @pl.when(first)
    def _():
        gate[...] = total.astype(BF16)

    @pl.when(jnp.logical_not(first))
    def _():
        up[...] = total.astype(BF16)


def grad_weights(part, pairs, width):
    depth, tokens = part.shape
    steps = depth // 512
    delta = pl.BlockSpec((tokens, width), lambda i: (0, 1 + i // steps))
    out = shape((depth, width), BF16)
    return _call(
        functools.partial(_grad_up_body, steps),
        (out, out, TICK),
        WHOLE,
        grid=(2 * steps,),
        in_specs=[pl.BlockSpec((512, tokens), lambda i: (lax.rem(i, steps), 0))] + [delta] * 2,
        out_specs=(
            pl.BlockSpec((512, width), lambda i: (jnp.minimum(i, steps - 1), 0)),
            pl.BlockSpec((512, width), lambda i: (jnp.maximum(i - steps, 0), 0)),
            _whole(8, 128),
        ),
        cost_estimate=_cost(
            flops=COST * 8 * tokens * depth * width, bytes_accessed=COST * 8 * depth * width, transcendentals=0
        ),
    )(part, *pairs)


def _grad_down_body(g, h0, h1, out, tick, turned):
    tick[...] = jnp.zeros_like(tick)

    @pl.when(pl.program_id(0) == 0)
    def _():
        for i, h in enumerate((h0, h1)):
            turned[i] = h[...].T

    rows, dims = g[...], (((1,), (1,)), ((), ()))
    total = lax.dot_general(turned[0], _twice(rows, 0), dims, preferred_element_type=F32)
    total = total + lax.dot_general(turned[1], _twice(rows, 1), dims, preferred_element_type=F32)
    out[...] = total.astype(BF16)


def grad_down_weight(part, pairs, width):
    depth, tokens = part.shape
    hidden = pl.BlockSpec((tokens, width), lambda i: (0, 0))
    return _call(
        _grad_down_body,
        (shape((width, depth), BF16), TICK),
        WHOLE,
        grid=(depth // 512,),
        in_specs=[pl.BlockSpec((512, tokens), lambda i: (i, 0))] + [hidden] * 2,
        out_specs=(pl.BlockSpec((width, 512), lambda i: (0, i)), _whole(8, 128)),
        scratch_shapes=[pltpu.VMEM((2, width, tokens), BF16)],
        cost_estimate=_cost(
            flops=COST * 4 * tokens * depth * width, bytes_accessed=COST * 4 * depth * width, transcendentals=0
        ),
    )(part, *pairs)


def _sum_first_body(ids, own, r1, r2, r3, _, own2, c1, c2, c3, tops):
    s2 = ids[3]
    for c in range(2):
        scales = [r[c, 512:528, :].astype(F32) for r in (r1, r2, r3)]
        for j in range(8):
            rows = slice(j * 64, (j + 1) * 64)
            total = own[c, rows, :]
            for r, scale in zip((r1, r2, r3), scales):
                total = total + _unpack(r[c, rows, :], scale[j : j + 1])
            y, place = j // 4, j % 4
            k = lax.rem(place - s2 + 4, 4)
            code, scale = _pack(total)
            tops[pl.ds(k, 1), y : y + 1, :] = scale[None]
            to = slice(y * 64, (y + 1) * 64)

            @pl.when(k == 0)
            def _():
                own2[c, to, :] = total

            for n, out in ((1, c1), (2, c2), (3, c3)):

                @pl.when(k == n)
                def _():
                    out[c, to, :] = code

        for n, out in ((1, c1), (2, c2), (3, c3)):
            out[c, 128:144, :] = jnp.concatenate([tops[n], tops[n]], axis=0).astype(BF16)


def sum_first(ids, own, received, after):
    tokens = own.shape[2]
    code = shape((2, 144, tokens), BF16)
    return _call(
        _sum_first_body,
        (shape((2, 128, tokens), F32), code, code, code),
        in_specs=[SMEM] + [VMEM] * 4 + [ANY],
        out_specs=(VMEM,) * 4,
        scratch_shapes=[pltpu.VMEM((4, 8, tokens), F32)],
    )(ids, own, *received, after)


def _sum_second_body(ids, own, r1, r2, r3, _, own3, out):
    for c in range(2):
        scales = [r[c, 128:144, :].astype(F32) for r in (r1, r2, r3)]
        for y in range(2):
            rows = slice(y * 64, (y + 1) * 64)
            total = own[c, rows, :]
            for r, scale in zip((r1, r2, r3), scales):
                total = total + _unpack(r[c, rows, :], scale[y : y + 1])

            @pl.when(ids[1] == y)
            def _():
                own3[c] = total

            @pl.when(ids[1] != y)
            def _():
                code, top = _pack(total)
                out[c, 0:64, :] = code
                out[c, 64:80, :] = jnp.broadcast_to(top, (16, top.shape[1])).astype(BF16)


def sum_second(ids, own, received, after):
    tokens = own.shape[2]
    return _call(
        _sum_second_body,
        (shape((2, 64, tokens), F32), shape((2, 80, tokens), BF16)),
        in_specs=[SMEM] + [VMEM] * 4 + [ANY],
        out_specs=(VMEM,) * 2,
    )(ids, own, *received, after)


def _sum_last_body(own, r, out):
    tokens = own.shape[2]
    for c in range(2):
        total = own[c] + _unpack(r[c, 0:64, :], r[c, 64:80, :].astype(F32)[0:1])
        out[:, c * tokens : (c + 1) * tokens] = total.astype(BF16)


def sum_last(own, received):
    return _call(
        _sum_last_body, shape((64, 2 * own.shape[2]), BF16), in_specs=[VMEM] * 2, out_specs=VMEM
    )(own, received)


def per_device(inputs, grad_out, gate_weight, up_weight, down_weight):
    width = gate_weight.shape[1]
    mp = lax.axis_index("mp")
    core = lax.axis_index("dp") % 2
    y, z, x = mp // 16, (mp // 4) % 4, mp % 4
    ids = jnp.stack([core, y, jnp.where(core == 0, x, z), jnp.where(core == 0, z, x)]).astype(jnp.int32)
    both = jnp.stack([inputs.T, grad_out.T])
    pair = jnp.stack([both, _send(both, _over_y)])
    near = [pair] + [_send(pair, _first(-k)) for k in (1, 2, 3)]
    x, g = (jnp.stack([p[:, i] for p in near]) for i in range(2))
    x1, x3 = _send(x, _second(-1)), _send(x, _second(1))
    x2 = _send(x1, _second(-1))
    g3, g1 = _send(g, _second(1)), _send(g, _second(-1))
    g2 = _send(g3, _second(1))

    def exchange(mine, others):
        chip, code, tick = chip_sum(mine, [_send(v, _over_core) for v in others])
        return (chip, _send(code, _over_lo)), tick

    *ups, x_acts = forward(ids, (x, x1, x2, x3), (gate_weight, up_weight), width)
    ups = [exchange(*part)[0] for part in ups]
    *downs, g_acts = forward(ids, (g, g1, g2, g3), (down_weight,), width)
    downs = [exchange(*part) for part in downs]
    tick = downs[1][1]
    pairs, part = [], ()
    for c in range(2):
        act = activations(*ups[c], *downs[c][0], tick)
        others = [_send(v, _over_core) for v in act]
        delta, *part, tick = grad_in(ids, gate_weight, up_weight, act, others, part)
        pairs.append(delta)
    own, *rest = part
    grad_gate, grad_up, tick = grad_weights(x_acts, pairs, width)
    own, *rest = sum_first(ids, own, [_send(v, _first(k + 1)) for k, v in enumerate(rest)], tick)
    grad_down, tick = grad_down_weight(g_acts, pairs, width)
    own, last = sum_second(ids, own, [_send(v, _second(k + 1)) for k, v in enumerate(rest)], tick)
    grad_inputs = sum_last(own, _send(last, _over_y)).T
    return (grad_inputs, grad_gate, grad_up, grad_down)


def solution(mesh):
    placed = (
        P(None, ("dp", "mp")),
        P(None, ("dp", "mp")),
        P("dp", "mp"),
        P("dp", "mp"),
        P("mp", "dp"),
    )
    return jax.shard_map(
        per_device,
        mesh=mesh,
        in_specs=placed,
        out_specs=(P(None, ("dp", "mp")), P("dp", "mp"), P("dp", "mp"), P("mp", "dp")),
        check_vma=False,
    )
```

```python
import functools

import jax
import jax.numpy as jnp
from jax import lax
from jax.experimental import pallas as pl
from jax.experimental.pallas import tpu as pltpu
from jax.sharding import PartitionSpec as P

COST = 20
F32, BF16 = jnp.float32, jnp.bfloat16
SMALL, DELTA, WHOLE = 16 * 1024 * 1024, 40 * 1024 * 1024, 60 * 1024 * 1024
BOTH = ("dp", "mp")


def _moves(shift):
    pairs = []
    for i in range(128):
        lo, core, y, z, x = i // 64, (i // 32) % 2, (i // 16) % 2, (i // 4) % 4, i % 4
        lo, core, y, z, x = shift(lo, core, y, z, x)
        pairs.append((i, (lo % 2) * 64 + (core % 2) * 32 + (y % 2) * 16 + (z % 4) * 4 + x % 4))
    return pairs


def _send(a, shift):
    return lax.ppermute(a, BOTH, _moves(shift))


def _first(k):
    return lambda lo, c, y, z, x: (lo, c, y, z + k * c, x + k * (1 - c))


def _second(k):
    return lambda lo, c, y, z, x: (lo, c, y, z + k * (1 - c), x + k * c)


def _over_y(lo, c, y, z, x):
    return lo, c, y + 1, z, x


def _over_core(lo, c, y, z, x):
    return lo, c + 1, y, z, x


def _over_lo(lo, c, y, z, x):
    return lo + 1, c, y, z, x


def encode(u, positive):
    code = jnp.exp2(u * 200.0 - 100.0)
    return jnp.where(positive, code, -code).astype(BF16)


def decode(code):
    wide = code.astype(F32)
    return (jnp.log2(jnp.abs(wide)) + 100.0) * (1.0 / 200.0), wide > 0


def _signed(value, positive):
    return jnp.where(positive, value, -value)


def _call(body, out, room=SMALL, **kw):
    params = pltpu.CompilerParams(vmem_limit_bytes=room)
    return pl.pallas_call(body, out_shape=out, compiler_params=params, **kw)


def _cost(flops, bytes_accessed, transcendentals):
    return pl.CostEstimate(
        flops=flops // COST, bytes_accessed=bytes_accessed // COST, transcendentals=transcendentals // COST
    )


SMEM = pl.BlockSpec(memory_space=pltpu.SMEM)
VMEM = pl.BlockSpec(memory_space=pltpu.VMEM)
ANY = pl.BlockSpec(memory_space=pl.ANY)


def shape(dims, dtype):
    return jax.ShapeDtypeStruct(dims, dtype)


TICK = shape((8, 128), F32)


def _forward_body(n, width, ids, *rest):
    pieces, weights, rest = rest[:4], rest[4 : 4 + n], rest[4 + n :]
    mine, theirs, rest = rest[:2], rest[2 : 2 + 2 * n], rest[2 + 2 * n :]
    acts_out, acts, turned, held, sums, loads, stores, sems = rest
    loading = [pltpu.make_async_copy(weight, held.at[i], loads.at[i]) for i, weight in enumerate(weights)]
    core, y, s1, s2 = ids[0], ids[1], ids[2], ids[3]
    copies = []
    for k2, piece in enumerate(pieces):
        b = lax.rem(s2 + k2, 4)
        for k1 in range(4):
            a = lax.rem(s1 + k1, 4)
            zx = jnp.where(core == 0, b * 4 + a, a * 4 + b)
            for k0 in range(2):
                at = pl.multiple_of((lax.rem(y + k0, 2) * 16 + zx) * 64, 64)
                copies.append(
                    pltpu.make_async_copy(piece.at[k1, k0], acts.at[pl.ds(at, 64), :], sems.at[len(copies)])
                )
    for copy in copies:
        copy.start()
    for copy in loading:
        copy.start()
    for copy in copies:
        copy.wait()
    out = [pltpu.make_async_copy(acts, acts_out, stores.at[0])]
    out[0].start()
    half = mine[0].shape[0]
    for m, place in enumerate((core, 1 - core)):
        for c in range(2):
            cols = pl.ds(pl.multiple_of((2 * c + place) * half, half), half)
            row = (2 * m + c) * half
            turned[row : row + half, :] = acts[:, cols].T
    for i in range(n):
        loading[i].wait()
        dims = (((1,), (0,)), ((), ())) if n == 2 else (((1,), (1,)), ((), ()))
        sums[i] = lax.dot_general(turned[...], held[i], dims, preferred_element_type=F32)
        for c in range(2):
            for row, to in (
                (c * half, mine[c].at[:, pl.ds(i * width, width)]),
                ((2 + c) * half, theirs[n * c + i]),
            ):
                copy = pltpu.make_async_copy(sums.at[i, pl.ds(row, half), :], to, stores.at[len(out)])
                copy.start()
                out.append(copy)
    for copy in out:
        copy.wait()


def _whole(*dims):
    return pl.BlockSpec(dims, lambda i: (0,) * len(dims))


def forward(ids, pieces, weights, width):
    n, tokens = len(weights), pieces[0].shape[-1]
    depth = 32 * 64
    mine, other = shape((tokens // 4, n * width), F32), shape((tokens // 4, width), F32)
    *out, acts = _call(
        functools.partial(_forward_body, n, width),
        (mine,) * 2 + (other,) * (2 * n) + (shape((depth, tokens), BF16),),
        WHOLE,
        in_specs=[SMEM] + [ANY] * (4 + n),
        out_specs=(ANY,) * (3 + 2 * n),
        scratch_shapes=[
            pltpu.VMEM((depth, tokens), BF16),
            pltpu.VMEM((tokens, depth), BF16),
            pltpu.VMEM((n, *weights[0].shape), BF16),
            pltpu.VMEM((n, tokens, width), F32),
            pltpu.SemaphoreType.DMA((n,)),
            pltpu.SemaphoreType.DMA((1 + 4 * n,)),
            pltpu.SemaphoreType.DMA((32,)),
        ],
        cost_estimate=_cost(
            flops=2 * n * tokens * depth * width, bytes_accessed=2 * n * depth * width + 4 * depth * tokens, transcendentals=0
        ),
    )(ids, *pieces, *weights)
    return (out[0], out[2 : 2 + n]), (out[1], out[2 + n :]), acts


def _chip_body(n, width, mine, *rest):
    others, (chip, code, tick) = rest[:n], rest[n:]
    tick[...] = jnp.zeros_like(tick)
    for i in range(n):
        cols = slice(i * width, (i + 1) * width)
        total = mine[:, cols] + others[i][...]
        chip[:, cols] = total
        size = jnp.abs(total)
        top = jnp.max(jnp.max(size, axis=0, keepdims=True), axis=1, keepdims=True)
        top = jnp.maximum(top * 1.01, 1e-35).astype(BF16).astype(F32)
        code[:, cols] = encode(jnp.sqrt(size * (1.0 / top)), total >= 0)
        code[16 * i : 16 * i + 16, n * width :] = jnp.broadcast_to(top, (16, 128)).astype(BF16)
    code[16 * n :, n * width :] = jnp.zeros((code.shape[0] - 16 * n, 128), BF16)


def chip_sum(mine, others):
    (rows, whole), n = mine.shape, len(others)
    return _call(
        functools.partial(_chip_body, n, whole // n),
        (shape((rows, whole), F32), shape((rows, whole + 128), BF16), TICK),
        in_specs=[VMEM] * (1 + n),
        out_specs=(VMEM,) * 3,
        cost_estimate=_cost(
            flops=20 * rows * whole, bytes_accessed=14 * rows * whole, transcendentals=2 * rows * whole
        ),
    )(mine, *others)


def _act_body(width, chip, code, chip_h, code_h, _, o0, o1, o2):
    def total(part, coded, i, n):
        cols = slice(i * width, (i + 1) * width)
        u, positive = decode(coded[:, cols])
        top = coded[16 * i : 16 * i + 16, n * width :].astype(F32)[0:1, 0:1]
        return part[:, cols] + _signed(u * u * top, positive)

    gate, up, grad_hidden = total(chip, code, 0, 2), total(chip, code, 1, 2), total(chip_h, code_h, 0, 1)
    squash = 1.0 / (1.0 + jnp.exp(-gate))
    o0[...] = gate * squash * up
    o1[...] = grad_hidden * up * squash * (1.0 + gate * (1.0 - squash))
    o2[...] = grad_hidden * gate * squash


def activations(chip, code, chip_h, code_h, after):
    rows, width = chip_h.shape
    return _call(
        functools.partial(_act_body, width),
        (shape((rows, width), F32),) * 3,
        in_specs=[VMEM] * 4 + [ANY],
        out_specs=(VMEM,) * 3,
        cost_estimate=_cost(
            flops=60 * rows * width, bytes_accessed=30 * rows * width, transcendentals=6 * rows * width
        ),
    )(chip, code, chip_h, code_h, after)


def _pack(block):
    size = jnp.abs(block)
    top = jnp.maximum(jnp.max(size, axis=0, keepdims=True) * 1.01, 1e-35)
    top = top.astype(BF16).astype(F32)
    return encode(size * (1.0 / top), block >= 0), top


def _unpack(code, top):
    u, positive = decode(code)
    return _signed(u * top, positive)


def _grad_in_body(width, n_before, ids, wg, wu, m0, m1, m2, o0, o1, o2, *rest):
    before, (pair_out, own, c1, c2, c3, tick, pair, right, tops, blocks, codes, sem, moves) = rest[:n_before], rest[n_before:]
    core, s1 = ids[0], ids[2]
    half = m0.shape[0]
    tokens = 2 * half
    tick[...] = jnp.zeros_like(tick)
    for parts, place in (((m0, m1, m2), core), ((o0, o1, o2), 1 - core)):
        rows = pl.ds(pl.multiple_of(place * half, half), half)
        rest = pl.ds(pl.multiple_of(tokens + place * half, half), half)
        for i, part in enumerate(parts):
            value = part[...]
            high = value.astype(BF16)
            low = (value - high.astype(F32)).astype(BF16)
            pair[rows, i * width : (i + 1) * width] = high
            pair[rest, i * width : (i + 1) * width] = low
            if i:
                right[rows, (2 * i - 2) * width : (2 * i - 1) * width] = high
                right[rows, (2 * i - 1) * width : 2 * i * width] = low
    store = [pltpu.make_async_copy(pair, pair_out, sem)]
    for i, (out, earlier) in enumerate(zip((own, c1, c2, c3), before)):
        store.append(pltpu.make_async_copy(earlier.at[0], out.at[0], moves.at[i]))
    for copy in store:
        copy.start()
    for part in range(4):
        some = slice(part * 512, (part + 1) * 512)
        g, u = wg[some, :], wu[some, :]
        total = lax.dot_general(
            jnp.concatenate([g, g, u, u], axis=1), right[...], (((1,), (1,)), ((), ())), preferred_element_type=F32
        )
        for sub in range(8):
            at, x = part * 2 + sub // 4, sub % 4
            y, z = at // 4, at % 4
            block = total[sub * 64 : (sub + 1) * 64]
            k = lax.rem(jnp.where(core == 0, x, z) - s1 + 4, 4)
            j = jnp.where(core == 0, at, y * 4 + x)
            rows = pl.ds(pl.multiple_of(j * 64, 64), 64)
            code, scale = _pack(block)
            tops[pl.ds(k, 1), pl.ds(j, 1), :] = scale[None]
            blocks[pl.ds(k, 1), rows, :] = block[None]
            codes[pl.ds(k, 1), rows, :] = code[None]
    c = own.shape[0] - 1
    own[c] = blocks[0]
    for n, out in ((1, c1), (2, c2), (3, c3)):
        out[c, 0:512, :] = codes[n]
        out[c, 512:528, :] = jnp.concatenate([tops[n], tops[n]], axis=0).astype(BF16)
    for copy in store:
        copy.wait()


def grad_in(ids, wg, wu, mine, theirs, before):
    half, width = mine[0].shape
    tokens, three = 2 * half, 3 * width
    n = 1 + (len(before) > 0)
    code = shape((n, 528, tokens), BF16)
    return _call(
        functools.partial(_grad_in_body, width, len(before)),
        (shape((2 * tokens, three), BF16), shape((n, 512, tokens), F32), code, code, code, TICK),
        DELTA,
        in_specs=[SMEM] + [VMEM] * (8 + len(before)),
        out_specs=(ANY,) + (VMEM,) * 5,
        scratch_shapes=[
            pltpu.VMEM((2 * tokens, three), BF16),
            pltpu.VMEM((tokens, 4 * width), BF16),
            pltpu.VMEM((4, 8, tokens), F32),
            pltpu.VMEM((4, 512, tokens), F32),
            pltpu.VMEM((4, 512, tokens), BF16),
            pltpu.SemaphoreType.DMA,
            pltpu.SemaphoreType.DMA((4,)),
        ],
        cost_estimate=_cost(
            flops=8 * tokens * 2048 * width, bytes_accessed=4 * 2048 * width + 16 * tokens * three, transcendentals=2048 * tokens
        ),
    )(ids, wg, wu, *mine, *theirs, *before)


def _twice(rows, c):
    half = rows.shape[1] // 2
    part = rows[:, c * half : (c + 1) * half]
    return jnp.concatenate([part, part], axis=1)


def _grad_up_body(steps, x, d0, d1, gate, up, tick):
    tick[...] = jnp.zeros_like(tick)
    rows = x[...]
    total = jnp.dot(_twice(rows, 0), d0[...], preferred_element_type=F32)
    total = total + jnp.dot(_twice(rows, 1), d1[...], preferred_element_type=F32)
    first = pl.program_id(0) < steps

    @pl.when(first)
    def _():
        gate[...] = total.astype(BF16)

    @pl.when(jnp.logical_not(first))
    def _():
        up[...] = total.astype(BF16)


def grad_weights(part, pairs, width):
    depth, tokens = part.shape
    steps = depth // 512
    delta = pl.BlockSpec((tokens, width), lambda i: (0, 1 + i // steps))
    out = shape((depth, width), BF16)
    return _call(
        functools.partial(_grad_up_body, steps),
        (out, out, TICK),
        DELTA,
        grid=(2 * steps,),
        in_specs=[pl.BlockSpec((512, tokens), lambda i: (lax.rem(i, steps), 0))] + [delta] * 2,
        out_specs=(
            pl.BlockSpec((512, width), lambda i: (jnp.minimum(i, steps - 1), 0)),
            pl.BlockSpec((512, width), lambda i: (jnp.maximum(i - steps, 0), 0)),
            _whole(8, 128),
        ),
        cost_estimate=_cost(
            flops=COST * 8 * tokens * depth * width, bytes_accessed=COST * 8 * depth * width, transcendentals=0
        ),
    )(part, *pairs)


def _grad_down_body(g, h0, h1, out, tick, turned):
    tick[...] = jnp.zeros_like(tick)

    @pl.when(pl.program_id(0) == 0)
    def _():
        for i, h in enumerate((h0, h1)):
            turned[i] = h[...].T

    rows, dims = g[...], (((1,), (1,)), ((), ()))
    total = lax.dot_general(turned[0], _twice(rows, 0), dims, preferred_element_type=F32)
    total = total + lax.dot_general(turned[1], _twice(rows, 1), dims, preferred_element_type=F32)
    out[...] = total.astype(BF16)


def grad_down_weight(part, pairs, width):
    depth, tokens = part.shape
    hidden = pl.BlockSpec((tokens, width), lambda i: (0, 0))
    return _call(
        _grad_down_body,
        (shape((width, depth), BF16), TICK),
        DELTA,
        grid=(depth // 512,),
        in_specs=[pl.BlockSpec((512, tokens), lambda i: (i, 0))] + [hidden] * 2,
        out_specs=(pl.BlockSpec((width, 512), lambda i: (0, i)), _whole(8, 128)),
        scratch_shapes=[pltpu.VMEM((2, width, tokens), BF16)],
        cost_estimate=_cost(
            flops=COST * 4 * tokens * depth * width, bytes_accessed=COST * 4 * depth * width, transcendentals=0
        ),
    )(part, *pairs)


def _sum_first_body(ids, own, r1, r2, r3, _, own2, c1, c2, c3, tops):
    s2 = ids[3]
    for c in range(2):
        scales = [r[c, 512:528, :].astype(F32) for r in (r1, r2, r3)]
        for j in range(8):
            rows = slice(j * 64, (j + 1) * 64)
            total = own[c, rows, :]
            for r, scale in zip((r1, r2, r3), scales):
                total = total + _unpack(r[c, rows, :], scale[j : j + 1])
            y, place = j // 4, j % 4
            k = lax.rem(place - s2 + 4, 4)
            code, scale = _pack(total)
            tops[pl.ds(k, 1), y : y + 1, :] = scale[None]
            to = slice(y * 64, (y + 1) * 64)

            @pl.when(k == 0)
            def _():
                own2[c, to, :] = total

            for n, out in ((1, c1), (2, c2), (3, c3)):

                @pl.when(k == n)
                def _():
                    out[c, to, :] = code

        for n, out in ((1, c1), (2, c2), (3, c3)):
            out[c, 128:144, :] = jnp.concatenate([tops[n], tops[n]], axis=0).astype(BF16)


def sum_first(ids, own, received, after):
    tokens = own.shape[2]
    code = shape((2, 144, tokens), BF16)
    return _call(
        _sum_first_body,
        (shape((2, 128, tokens), F32), code, code, code),
        in_specs=[SMEM] + [VMEM] * 4 + [ANY],
        out_specs=(VMEM,) * 4,
        scratch_shapes=[pltpu.VMEM((4, 8, tokens), F32)],
    )(ids, own, *received, after)


def _sum_second_body(ids, own, r1, r2, r3, _, own3, out):
    for c in range(2):
        scales = [r[c, 128:144, :].astype(F32) for r in (r1, r2, r3)]
        for y in range(2):
            rows = slice(y * 64, (y + 1) * 64)
            total = own[c, rows, :]
            for r, scale in zip((r1, r2, r3), scales):
                total = total + _unpack(r[c, rows, :], scale[y : y + 1])

            @pl.when(ids[1] == y)
            def _():
                own3[c] = total

            @pl.when(ids[1] != y)
            def _():
                code, top = _pack(total)
                out[c, 0:64, :] = code
                out[c, 64:80, :] = jnp.broadcast_to(top, (16, top.shape[1])).astype(BF16)


def sum_second(ids, own, received, after):
    tokens = own.shape[2]
    return _call(
        _sum_second_body,
        (shape((2, 64, tokens), F32), shape((2, 80, tokens), BF16)),
        in_specs=[SMEM] + [VMEM] * 4 + [ANY],
        out_specs=(VMEM,) * 2,
    )(ids, own, *received, after)


def _sum_last_body(own, r, out):
    tokens = own.shape[2]
    for c in range(2):
        total = own[c] + _unpack(r[c, 0:64, :], r[c, 64:80, :].astype(F32)[0:1])
        out[:, c * tokens : (c + 1) * tokens] = total.astype(BF16)


def sum_last(own, received):
    return _call(
        _sum_last_body, shape((64, 2 * own.shape[2]), BF16), in_specs=[VMEM] * 2, out_specs=VMEM
    )(own, received)


def per_device(inputs, grad_out, gate_weight, up_weight, down_weight):
    width = gate_weight.shape[1]
    mp = lax.axis_index("mp")
    core = lax.axis_index("dp") % 2
    y, z, x = mp // 16, (mp // 4) % 4, mp % 4
    ids = jnp.stack([core, y, jnp.where(core == 0, x, z), jnp.where(core == 0, z, x)]).astype(jnp.int32)
    both = jnp.stack([inputs.T, grad_out.T])
    pair = jnp.stack([both, _send(both, _over_y)])
    near = [pair] + [_send(pair, _first(-k)) for k in (1, 2, 3)]
    x, g = (jnp.stack([p[:, i] for p in near]) for i in range(2))
    x1, x3 = _send(x, _second(-1)), _send(x, _second(1))
    x2 = _send(x1, _second(-1))
    g3, g1 = _send(g, _second(1)), _send(g, _second(-1))
    g2 = _send(g3, _second(1))

    def exchange(mine, others):
        chip, code, tick = chip_sum(mine, [_send(v, _over_core) for v in others])
        return (chip, _send(code, _over_lo)), tick

    *ups, x_acts = forward(ids, (x, x1, x2, x3), (gate_weight, up_weight), width)
    ups = [exchange(*part)[0] for part in ups]
    *downs, g_acts = forward(ids, (g, g1, g2, g3), (down_weight,), width)
    downs = [exchange(*part) for part in downs]
    tick = downs[1][1]
    pairs, part = [], ()
    for c in range(2):
        act = activations(*ups[c], *downs[c][0], tick)
        others = [_send(v, _over_core) for v in act]
        delta, *part, tick = grad_in(ids, gate_weight, up_weight, act, others, part)
        pairs.append(delta)
    own, *rest = part
    grad_gate, grad_up, tick = grad_weights(x_acts, pairs, width)
    own, *rest = sum_first(ids, own, [_send(v, _first(k + 1)) for k, v in enumerate(rest)], tick)
    grad_down, tick = grad_down_weight(g_acts, pairs, width)
    own, last = sum_second(ids, own, [_send(v, _second(k + 1)) for k, v in enumerate(rest)], tick)
    grad_inputs = sum_last(own, _send(last, _over_y)).T
    return (grad_inputs, grad_gate, grad_up, grad_down)


def solution(mesh):
    placed = (
        P(None, ("dp", "mp")),
        P(None, ("dp", "mp")),
        P("dp", "mp"),
        P("dp", "mp"),
        P("mp", "dp"),
    )
    return jax.shard_map(
        per_device,
        mesh=mesh,
        in_specs=placed,
        out_specs=(P(None, ("dp", "mp")), P("dp", "mp"), P("dp", "mp"), P("mp", "dp")),
        check_vma=False,
    )
```

```python
import functools

import jax
import jax.numpy as jnp
from jax import lax
from jax.experimental import pallas as pl
from jax.experimental.pallas import tpu as pltpu
from jax.sharding import PartitionSpec as P

COST = 20
F32, BF16 = jnp.float32, jnp.bfloat16
SMALL, DELTA, WHOLE = 16 * 1024 * 1024, 40 * 1024 * 1024, 60 * 1024 * 1024
BOTH = ("dp", "mp")


def _moves(shift):
    pairs = []
    for i in range(128):
        lo, core, y, z, x = i // 64, (i // 32) % 2, (i // 16) % 2, (i // 4) % 4, i % 4
        lo, core, y, z, x = shift(lo, core, y, z, x)
        pairs.append((i, (lo % 2) * 64 + (core % 2) * 32 + (y % 2) * 16 + (z % 4) * 4 + x % 4))
    return pairs


def _send(a, shift):
    return lax.ppermute(a, BOTH, _moves(shift))


def _first(k):
    return lambda lo, c, y, z, x: (lo, c, y, z + k * c, x + k * (1 - c))


def _second(k):
    return lambda lo, c, y, z, x: (lo, c, y, z + k * (1 - c), x + k * c)


def _over_y(lo, c, y, z, x):
    return lo, c, y + 1, z, x


def _over_core(lo, c, y, z, x):
    return lo, c + 1, y, z, x


def _over_lo(lo, c, y, z, x):
    return lo + 1, c, y, z, x


def encode(u, positive):
    code = jnp.exp2(u * 200.0 - 100.0)
    return jnp.where(positive, code, -code).astype(BF16)


def decode(code):
    wide = code.astype(F32)
    return (jnp.log2(jnp.abs(wide)) + 100.0) * (1.0 / 200.0), wide > 0


def _signed(value, positive):
    return jnp.where(positive, value, -value)


def _call(body, out, room=SMALL, **kw):
    params = pltpu.CompilerParams(vmem_limit_bytes=room)
    return pl.pallas_call(body, out_shape=out, compiler_params=params, **kw)


def _cost(flops, bytes_accessed, transcendentals):
    return pl.CostEstimate(
        flops=flops // COST, bytes_accessed=bytes_accessed // COST, transcendentals=transcendentals // COST
    )


SMEM = pl.BlockSpec(memory_space=pltpu.SMEM)
VMEM = pl.BlockSpec(memory_space=pltpu.VMEM)
ANY = pl.BlockSpec(memory_space=pl.ANY)


def shape(dims, dtype):
    return jax.ShapeDtypeStruct(dims, dtype)


TICK = shape((8, 128), F32)


def _forward_body(n, width, ids, *rest):
    pieces, weights, rest = rest[:4], rest[4 : 4 + n], rest[4 + n :]
    mine, theirs, rest = rest[:2], rest[2 : 2 + 2 * n], rest[2 + 2 * n :]
    acts_out, acts, turned, held, sums, loads, stores, sems = rest
    loading = [pltpu.make_async_copy(weight, held.at[i], loads.at[i]) for i, weight in enumerate(weights)]
    core, y, s1, s2 = ids[0], ids[1], ids[2], ids[3]
    copies = []
    for k2, piece in enumerate(pieces):
        b = lax.rem(s2 + k2, 4)
        for k1 in range(4):
            a = lax.rem(s1 + k1, 4)
            zx = jnp.where(core == 0, b * 4 + a, a * 4 + b)
            for k0 in range(2):
                at = pl.multiple_of((lax.rem(y + k0, 2) * 16 + zx) * 64, 64)
                copies.append(
                    pltpu.make_async_copy(piece.at[k1, k0], acts.at[pl.ds(at, 64), :], sems.at[len(copies)])
                )
    for copy in copies:
        copy.start()
    for copy in loading:
        copy.start()
    for copy in copies:
        copy.wait()
    out = [pltpu.make_async_copy(acts, acts_out, stores.at[0])]
    out[0].start()
    half = mine[0].shape[0]
    for m, place in enumerate((core, 1 - core)):
        for c in range(2):
            cols = pl.ds(pl.multiple_of((2 * c + place) * half, half), half)
            row = (2 * m + c) * half
            turned[row : row + half, :] = acts[:, cols].T
    for i in range(n):
        loading[i].wait()
        dims = (((1,), (0,)), ((), ())) if n == 2 else (((1,), (1,)), ((), ()))
        sums[i] = lax.dot_general(turned[...], held[i], dims, preferred_element_type=F32)
        for c in range(2):
            for row, to in (
                (c * half, mine[c].at[:, pl.ds(i * width, width)]),
                ((2 + c) * half, theirs[n * c + i]),
            ):
                copy = pltpu.make_async_copy(sums.at[i, pl.ds(row, half), :], to, stores.at[len(out)])
                copy.start()
                out.append(copy)
    for copy in out:
        copy.wait()


def _whole(*dims):
    return pl.BlockSpec(dims, lambda i: (0,) * len(dims))


def forward(ids, pieces, weights, width):
    n, tokens = len(weights), pieces[0].shape[-1]
    depth = 32 * 64
    mine, other = shape((tokens // 4, n * width), F32), shape((tokens // 4, width), F32)
    *out, acts = _call(
        functools.partial(_forward_body, n, width),
        (mine,) * 2 + (other,) * (2 * n) + (shape((depth, tokens), BF16),),
        DELTA if n == 1 else WHOLE,
        in_specs=[SMEM] + [ANY] * (4 + n),
        out_specs=(ANY,) * (3 + 2 * n),
        scratch_shapes=[
            pltpu.VMEM((depth, tokens), BF16),
            pltpu.VMEM((tokens, depth), BF16),
            pltpu.VMEM((n, *weights[0].shape), BF16),
            pltpu.VMEM((n, tokens, width), F32),
            pltpu.SemaphoreType.DMA((n,)),
            pltpu.SemaphoreType.DMA((1 + 4 * n,)),
            pltpu.SemaphoreType.DMA((32,)),
        ],
        cost_estimate=_cost(
            flops=2 * n * tokens * depth * width, bytes_accessed=2 * n * depth * width + 4 * depth * tokens, transcendentals=0
        ),
    )(ids, *pieces, *weights)
    return (out[0], out[2 : 2 + n]), (out[1], out[2 + n :]), acts


def _chip_body(n, width, mine, *rest):
    others, (chip, code, tick) = rest[:n], rest[n:]
    tick[...] = jnp.zeros_like(tick)
    for i in range(n):
        cols = slice(i * width, (i + 1) * width)
        total = mine[:, cols] + others[i][...]
        chip[:, cols] = total
        size = jnp.abs(total)
        top = jnp.max(jnp.max(size, axis=0, keepdims=True), axis=1, keepdims=True)
        top = jnp.maximum(top * 1.01, 1e-35).astype(BF16).astype(F32)
        code[:, cols] = encode(jnp.sqrt(size * (1.0 / top)), total >= 0)
        code[16 * i : 16 * i + 16, n * width :] = jnp.broadcast_to(top, (16, 128)).astype(BF16)
    code[16 * n :, n * width :] = jnp.zeros((code.shape[0] - 16 * n, 128), BF16)


def chip_sum(mine, others):
    (rows, whole), n = mine.shape, len(others)
    return _call(
        functools.partial(_chip_body, n, whole // n),
        (shape((rows, whole), F32), shape((rows, whole + 128), BF16), TICK),
        in_specs=[VMEM] * (1 + n),
        out_specs=(VMEM,) * 3,
        cost_estimate=_cost(
            flops=20 * rows * whole, bytes_accessed=14 * rows * whole, transcendentals=2 * rows * whole
        ),
    )(mine, *others)


def _act_body(width, chip, code, chip_h, code_h, _, o0, o1, o2):
    def total(part, coded, i, n):
        cols = slice(i * width, (i + 1) * width)
        u, positive = decode(coded[:, cols])
        top = coded[16 * i : 16 * i + 16, n * width :].astype(F32)[0:1, 0:1]
        return part[:, cols] + _signed(u * u * top, positive)

    gate, up, grad_hidden = total(chip, code, 0, 2), total(chip, code, 1, 2), total(chip_h, code_h, 0, 1)
    squash = 1.0 / (1.0 + jnp.exp(-gate))
    o0[...] = gate * squash * up
    o1[...] = grad_hidden * up * squash * (1.0 + gate * (1.0 - squash))
    o2[...] = grad_hidden * gate * squash


def activations(chip, code, chip_h, code_h, after):
    rows, width = chip_h.shape
    return _call(
        functools.partial(_act_body, width),
        (shape((rows, width), F32),) * 3,
        in_specs=[VMEM] * 4 + [ANY],
        out_specs=(VMEM,) * 3,
        cost_estimate=_cost(
            flops=60 * rows * width, bytes_accessed=30 * rows * width, transcendentals=6 * rows * width
        ),
    )(chip, code, chip_h, code_h, after)


def _pack(block):
    size = jnp.abs(block)
    top = jnp.maximum(jnp.max(size, axis=0, keepdims=True) * 1.01, 1e-35)
    top = top.astype(BF16).astype(F32)
    return encode(size * (1.0 / top), block >= 0), top


def _unpack(code, top):
    u, positive = decode(code)
    return _signed(u * top, positive)


def _grad_in_body(width, n_before, ids, wg, wu, m0, m1, m2, o0, o1, o2, *rest):
    before, (pair_out, own, c1, c2, c3, tick, pair, right, tops, blocks, codes, sem, moves) = rest[:n_before], rest[n_before:]
    core, s1 = ids[0], ids[2]
    half = m0.shape[0]
    tokens = 2 * half
    tick[...] = jnp.zeros_like(tick)
    for parts, place in (((m0, m1, m2), core), ((o0, o1, o2), 1 - core)):
        rows = pl.ds(pl.multiple_of(place * half, half), half)
        rest = pl.ds(pl.multiple_of(tokens + place * half, half), half)
        for i, part in enumerate(parts):
            value = part[...]
            high = value.astype(BF16)
            low = (value - high.astype(F32)).astype(BF16)
            pair[rows, i * width : (i + 1) * width] = high
            pair[rest, i * width : (i + 1) * width] = low
            if i:
                right[rows, (2 * i - 2) * width : (2 * i - 1) * width] = high
                right[rows, (2 * i - 1) * width : 2 * i * width] = low
    store = [pltpu.make_async_copy(pair, pair_out, sem)]
    for i, (out, earlier) in enumerate(zip((own, c1, c2, c3), before)):
        store.append(pltpu.make_async_copy(earlier.at[0], out.at[0], moves.at[i]))
    for copy in store:
        copy.start()
    for part in range(4):
        some = slice(part * 512, (part + 1) * 512)
        g, u = wg[some, :], wu[some, :]
        total = lax.dot_general(
            jnp.concatenate([g, g, u, u], axis=1), right[...], (((1,), (1,)), ((), ())), preferred_element_type=F32
        )
        for sub in range(8):
            at, x = part * 2 + sub // 4, sub % 4
            y, z = at // 4, at % 4
            block = total[sub * 64 : (sub + 1) * 64]
            k = lax.rem(jnp.where(core == 0, x, z) - s1 + 4, 4)
            j = jnp.where(core == 0, at, y * 4 + x)
            rows = pl.ds(pl.multiple_of(j * 64, 64), 64)
            code, scale = _pack(block)
            tops[pl.ds(k, 1), pl.ds(j, 1), :] = scale[None]
            blocks[pl.ds(k, 1), rows, :] = block[None]
            codes[pl.ds(k, 1), rows, :] = code[None]
    c = own.shape[0] - 1
    own[c] = blocks[0]
    for n, out in ((1, c1), (2, c2), (3, c3)):
        out[c, 0:512, :] = codes[n]
        out[c, 512:528, :] = jnp.concatenate([tops[n], tops[n]], axis=0).astype(BF16)
    for copy in store:
        copy.wait()


def grad_in(ids, wg, wu, mine, theirs, before):
    half, width = mine[0].shape
    tokens, three = 2 * half, 3 * width
    n = 1 + (len(before) > 0)
    code = shape((n, 528, tokens), BF16)
    return _call(
        functools.partial(_grad_in_body, width, len(before)),
        (shape((2 * tokens, three), BF16), shape((n, 512, tokens), F32), code, code, code, TICK),
        DELTA,
        in_specs=[SMEM] + [VMEM] * (8 + len(before)),
        out_specs=(ANY,) + (VMEM,) * 5,
        scratch_shapes=[
            pltpu.VMEM((2 * tokens, three), BF16),
            pltpu.VMEM((tokens, 4 * width), BF16),
            pltpu.VMEM((4, 8, tokens), F32),
            pltpu.VMEM((4, 512, tokens), F32),
            pltpu.VMEM((4, 512, tokens), BF16),
            pltpu.SemaphoreType.DMA,
            pltpu.SemaphoreType.DMA((4,)),
        ],
        cost_estimate=_cost(
            flops=8 * tokens * 2048 * width, bytes_accessed=4 * 2048 * width + 16 * tokens * three, transcendentals=2048 * tokens
        ),
    )(ids, wg, wu, *mine, *theirs, *before)


def _twice(rows, c):
    half = rows.shape[1] // 2
    part = rows[:, c * half : (c + 1) * half]
    return jnp.concatenate([part, part], axis=1)


def _grad_up_body(steps, x, d0, d1, gate, up, tick):
    tick[...] = jnp.zeros_like(tick)
    rows = x[...]
    total = jnp.dot(_twice(rows, 0), d0[...], preferred_element_type=F32)
    total = total + jnp.dot(_twice(rows, 1), d1[...], preferred_element_type=F32)
    first = pl.program_id(0) < steps

    @pl.when(first)
    def _():
        gate[...] = total.astype(BF16)

    @pl.when(jnp.logical_not(first))
    def _():
        up[...] = total.astype(BF16)


def grad_weights(part, pairs, width):
    depth, tokens = part.shape
    steps = depth // 512
    delta = pl.BlockSpec((tokens, width), lambda i: (0, 1 + i // steps))
    out = shape((depth, width), BF16)
    return _call(
        functools.partial(_grad_up_body, steps),
        (out, out, TICK),
        DELTA,
        grid=(2 * steps,),
        in_specs=[pl.BlockSpec((512, tokens), lambda i: (lax.rem(i, steps), 0))] + [delta] * 2,
        out_specs=(
            pl.BlockSpec((512, width), lambda i: (jnp.minimum(i, steps - 1), 0)),
            pl.BlockSpec((512, width), lambda i: (jnp.maximum(i - steps, 0), 0)),
            _whole(8, 128),
        ),
        cost_estimate=_cost(
            flops=COST * 8 * tokens * depth * width, bytes_accessed=COST * 8 * depth * width, transcendentals=0
        ),
    )(part, *pairs)


def _grad_down_body(g, h0, h1, out, tick, turned):
    tick[...] = jnp.zeros_like(tick)

    @pl.when(pl.program_id(0) == 0)
    def _():
        for i, h in enumerate((h0, h1)):
            turned[i] = h[...].T

    rows, dims = g[...], (((1,), (1,)), ((), ()))
    total = lax.dot_general(turned[0], _twice(rows, 0), dims, preferred_element_type=F32)
    total = total + lax.dot_general(turned[1], _twice(rows, 1), dims, preferred_element_type=F32)
    out[...] = total.astype(BF16)


def grad_down_weight(part, pairs, width):
    depth, tokens = part.shape
    hidden = pl.BlockSpec((tokens, width), lambda i: (0, 0))
    return _call(
        _grad_down_body,
        (shape((width, depth), BF16), TICK),
        DELTA,
        grid=(depth // 512,),
        in_specs=[pl.BlockSpec((512, tokens), lambda i: (i, 0))] + [hidden] * 2,
        out_specs=(pl.BlockSpec((width, 512), lambda i: (0, i)), _whole(8, 128)),
        scratch_shapes=[pltpu.VMEM((2, width, tokens), BF16)],
        cost_estimate=_cost(
            flops=COST * 4 * tokens * depth * width, bytes_accessed=COST * 4 * depth * width, transcendentals=0
        ),
    )(part, *pairs)


def _sum_first_body(ids, own, r1, r2, r3, _, own2, c1, c2, c3, tops):
    s2 = ids[3]
    for c in range(2):
        scales = [r[c, 512:528, :].astype(F32) for r in (r1, r2, r3)]
        for j in range(8):
            rows = slice(j * 64, (j + 1) * 64)
            total = own[c, rows, :]
            for r, scale in zip((r1, r2, r3), scales):
                total = total + _unpack(r[c, rows, :], scale[j : j + 1])
            y, place = j // 4, j % 4
            k = lax.rem(place - s2 + 4, 4)
            code, scale = _pack(total)
            tops[pl.ds(k, 1), y : y + 1, :] = scale[None]
            to = slice(y * 64, (y + 1) * 64)

            @pl.when(k == 0)
            def _():
                own2[c, to, :] = total

            for n, out in ((1, c1), (2, c2), (3, c3)):

                @pl.when(k == n)
                def _():
                    out[c, to, :] = code

        for n, out in ((1, c1), (2, c2), (3, c3)):
            out[c, 128:144, :] = jnp.concatenate([tops[n], tops[n]], axis=0).astype(BF16)


def sum_first(ids, own, received, after):
    tokens = own.shape[2]
    code = shape((2, 144, tokens), BF16)
    return _call(
        _sum_first_body,
        (shape((2, 128, tokens), F32), code, code, code),
        in_specs=[SMEM] + [VMEM] * 4 + [ANY],
        out_specs=(VMEM,) * 4,
        scratch_shapes=[pltpu.VMEM((4, 8, tokens), F32)],
    )(ids, own, *received, after)


def _sum_second_body(ids, own, r1, r2, r3, _, own3, out):
    for c in range(2):
        scales = [r[c, 128:144, :].astype(F32) for r in (r1, r2, r3)]
        for y in range(2):
            rows = slice(y * 64, (y + 1) * 64)
            total = own[c, rows, :]
            for r, scale in zip((r1, r2, r3), scales):
                total = total + _unpack(r[c, rows, :], scale[y : y + 1])

            @pl.when(ids[1] == y)
            def _():
                own3[c] = total

            @pl.when(ids[1] != y)
            def _():
                code, top = _pack(total)
                out[c, 0:64, :] = code
                out[c, 64:80, :] = jnp.broadcast_to(top, (16, top.shape[1])).astype(BF16)


def sum_second(ids, own, received, after):
    tokens = own.shape[2]
    return _call(
        _sum_second_body,
        (shape((2, 64, tokens), F32), shape((2, 80, tokens), BF16)),
        in_specs=[SMEM] + [VMEM] * 4 + [ANY],
        out_specs=(VMEM,) * 2,
    )(ids, own, *received, after)


def _sum_last_body(own, r, out):
    tokens = own.shape[2]
    for c in range(2):
        total = own[c] + _unpack(r[c, 0:64, :], r[c, 64:80, :].astype(F32)[0:1])
        out[:, c * tokens : (c + 1) * tokens] = total.astype(BF16)


def sum_last(own, received):
    return _call(
        _sum_last_body, shape((64, 2 * own.shape[2]), BF16), in_specs=[VMEM] * 2, out_specs=VMEM
    )(own, received)


def per_device(inputs, grad_out, gate_weight, up_weight, down_weight):
    width = gate_weight.shape[1]
    mp = lax.axis_index("mp")
    core = lax.axis_index("dp") % 2
    y, z, x = mp // 16, (mp // 4) % 4, mp % 4
    ids = jnp.stack([core, y, jnp.where(core == 0, x, z), jnp.where(core == 0, z, x)]).astype(jnp.int32)
    both = jnp.stack([inputs.T, grad_out.T])
    pair = jnp.stack([both, _send(both, _over_y)])
    near = [pair] + [_send(pair, _first(-k)) for k in (1, 2, 3)]
    x, g = (jnp.stack([p[:, i] for p in near]) for i in range(2))
    x1, x3 = _send(x, _second(-1)), _send(x, _second(1))
    x2 = _send(x1, _second(-1))
    g3, g1 = _send(g, _second(1)), _send(g, _second(-1))
    g2 = _send(g3, _second(1))

    def exchange(mine, others):
        chip, code, tick = chip_sum(mine, [_send(v, _over_core) for v in others])
        return (chip, _send(code, _over_lo)), tick

    *ups, x_acts = forward(ids, (x, x1, x2, x3), (gate_weight, up_weight), width)
    ups = [exchange(*part)[0] for part in ups]
    *downs, g_acts = forward(ids, (g, g1, g2, g3), (down_weight,), width)
    downs = [exchange(*part) for part in downs]
    tick = downs[1][1]
    pairs, part = [], ()
    for c in range(2):
        act = activations(*ups[c], *downs[c][0], tick)
        others = [_send(v, _over_core) for v in act]
        delta, *part, tick = grad_in(ids, gate_weight, up_weight, act, others, part)
        pairs.append(delta)
    own, *rest = part
    grad_gate, grad_up, tick = grad_weights(x_acts, pairs, width)
    own, *rest = sum_first(ids, own, [_send(v, _first(k + 1)) for k, v in enumerate(rest)], tick)
    grad_down, tick = grad_down_weight(g_acts, pairs, width)
    own, last = sum_second(ids, own, [_send(v, _second(k + 1)) for k, v in enumerate(rest)], tick)
    grad_inputs = sum_last(own, _send(last, _over_y)).T
    return (grad_inputs, grad_gate, grad_up, grad_down)


def solution(mesh):
    placed = (
        P(None, ("dp", "mp")),
        P(None, ("dp", "mp")),
        P("dp", "mp"),
        P("dp", "mp"),
        P("mp", "dp"),
    )
    return jax.shard_map(
        per_device,
        mesh=mesh,
        in_specs=placed,
        out_specs=(P(None, ("dp", "mp")), P("dp", "mp"), P("dp", "mp"), P("mp", "dp")),
        check_vma=False,
    )
```
